128 devices in a mesh: dom: 32 (over x, y, core), rep: 4 (over z).
Axes of the slice: x: 4, y: 4, z: 4, core: 2. Of those that a mesh axis runs over, the one named last changes fastest.
Arguments:
- features: bfloat16 [131072, 512], P(('dom', 'rep')), may hold values from -6 to 6
- w_self: bfloat16 [512, 512], replicated, may hold values from -0.25 to 0.25
- w_neigh: bfloat16 [512, 512], replicated, may hold values from -0.25 to 0.25
- local_tiles: bfloat16 [16384, 128, 128], P(('dom', 'rep')), may hold values from -0.09375 to 0.09375
- local_rows: int32 [16384], P(('dom', 'rep')), may hold values from 0 to 7
- local_cols: int32 [16384], P(('dom', 'rep')), may hold values from 0 to 31
- halo_tiles: bfloat16 [12288, 128, 128], P(('dom', 'rep')), may hold values from -0.09375 to 0.09375
- halo_rows: int32 [12288], P(('dom', 'rep')), may hold values from 0 to 7
- halo_cols: int32 [12288], P(('dom', 'rep')), may hold values from 0 to 15
- cut_rows: int32 [32, 4, 32, 64], P('dom', 'rep'), may hold values from 0 to 1023
- cut_counts: int32 [32, 4, 32], P('dom', 'rep'), may hold values from 0 to 64, as said below
- cotangent: bfloat16 [131072, 512], P(('dom', 'rep')), may hold values from -6 to 6
Outputs:
- out: bfloat16 [131072, 512], P(('dom', 'rep'))
- d_x: bfloat16 [131072, 512], P(('dom', 'rep'))
- d_w_self: float32 [512, 512], P('rep')
- d_w_neigh: float32 [512, 512], P('rep')
The draws below stay inside these ranges and needn't reach their ends.
Inputs may be any that keep to these rules, and one draw needn't show every extreme that they name: Each device sends 64 rows to at least one partition and none to its own partition; slots from cut_counts[p, r, q] on are unused.
All inputs are finite; a program needn't handle non-finite values.
Results may differ from the reference program's by a relative error of at most 0.008.
Values may be sent and summed in bfloat16 or wider, within the bound.
A program may use at most 128 MiB of HBM per device.

```python
import math
import jax
import jax.numpy as jnp
from jax import lax

D = 512
TB = 128
R = 1024
NL = 128
NH = 96
C = 64
RB = 8
PB = 32
HB = 16
NODES = 131072
N_DOM = 32
N_REP = 4


def draw_cut_counts(key, part):
    shape_full = (N_DOM, N_REP, N_DOM)
    drawn = jax.random.randint(key, shape_full, C // 8, C + 1)
    source_part = lax.broadcasted_iota(jnp.int32, shape_full, 0)
    target_part = lax.broadcasted_iota(jnp.int32, shape_full, 2)
    drawn = jnp.where(target_part == (source_part + 1) % N_DOM, C, drawn)
    drawn = jnp.where(target_part == source_part, 0, drawn)
    return drawn.astype(jnp.int32)


def place_ends(entries, own_key, smallest, top_value):
    spot = [jax.random.randint(jax.random.fold_in(own_key, axis), (), 0, length) for axis, length in enumerate(entries.shape)]
    main_axis = entries.shape.index(max(entries.shape))
    beside = spot[:main_axis] + [(spot[main_axis] + 1) % entries.shape[main_axis]] + spot[main_axis + 1:]
    return entries.at[tuple(spot)].set(smallest).at[tuple(beside)].set(top_value)


def levels(key, dims, pieces, smallest, top_value):
    gain = 1.0
    for axis_at, blocks in pieces:
        draws = jax.random.uniform(jax.random.fold_in(jax.random.fold_in(key, 6), axis_at), (blocks,), jnp.float32, smallest / len(pieces), top_value / len(pieces))
        gain = gain * jnp.repeat(jnp.exp(draws), dims[axis_at] // blocks).reshape((-1,) + (1,) * (len(dims) - 1 - axis_at))
    return gain


def scatter_about(stream_key, shape, spread, most, split=(), kind=jnp.bfloat16):
    values = spread * jax.random.normal(stream_key, shape, jnp.float32)
    if split:
        values = values * levels(stream_key, shape, split, -0.22, 0.18)
    return jnp.clip(values, -most, most).astype(kind)


def setup_inputs(seed: int = 0) -> dict:
    streams_of = jax.random.split(jax.random.key(seed), 13)
    return {
        "features": scatter_about(streams_of[0], (NODES, D), 1.0, 6.0, ((0, 128),)),
        "w_self": scatter_about(streams_of[1], (D, D), D ** -0.5, 0.25),
        "w_neigh": scatter_about(streams_of[2], (D, D), D ** -0.5, 0.25),
        "local_tiles": scatter_about(streams_of[3], (N_DOM * N_REP * NL, TB, TB), ((NL + NH) * TB // RB) ** -0.5, 0.09375, ((0, 128),)),
        "local_rows": place_ends(jax.random.randint(streams_of[4], (N_DOM * N_REP * NL,), 0, RB), jax.random.fold_in(streams_of[4], 1), 0, RB - 1).astype(jnp.int32),
        "local_cols": place_ends(jax.random.randint(streams_of[5], (N_DOM * N_REP * NL,), 0, PB), jax.random.fold_in(streams_of[5], 1), 0, PB - 1).astype(jnp.int32),
        "halo_tiles": scatter_about(streams_of[6], (N_DOM * N_REP * NH, TB, TB), ((NL + NH) * TB // RB) ** -0.5, 0.09375, ((0, 128),)),
        "halo_rows": place_ends(jax.random.randint(streams_of[7], (N_DOM * N_REP * NH,), 0, RB), jax.random.fold_in(streams_of[7], 1), 0, RB - 1).astype(jnp.int32),
        "halo_cols": place_ends(jax.random.randint(streams_of[8], (N_DOM * N_REP * NH,), 0, HB), jax.random.fold_in(streams_of[8], 1), 0, HB - 1).astype(jnp.int32),
        "cut_rows": place_ends(jax.random.randint(streams_of[9], (N_DOM, N_REP, N_DOM, C), 0, R), jax.random.fold_in(streams_of[9], 1), 0, R - 1).astype(jnp.int32),
        "cut_counts": draw_cut_counts(jax.random.fold_in(streams_of[12], 71), 0),
        "cotangent": scatter_about(streams_of[11], (NODES, D), 1.0, 6.0, ((0, 128),)),
    }


def aggregate(source, tiles, pick_index, place_index, out_blocks, transposed):
    tile_count = tiles.shape[0]
    group_size = math.gcd(tile_count, 32)
    tile_size = tiles.shape[1]
    feat_width = source.shape[2]
    grouped = tiles.reshape(tile_count // group_size, group_size, tile_size, tile_size)
    picks = pick_index.reshape(tile_count // group_size, group_size)
    places = place_index.reshape(tile_count // group_size, group_size)
    targets = jnp.arange(out_blocks, dtype=jnp.int32)

    def advance(running, scan_item):
        tile_block, pick_group, place_group = scan_item
        picked = jnp.take(source, pick_group, axis=0).astype(jnp.float32)
        tile_wide = tile_block.astype(jnp.float32)
        if transposed:
            products = jnp.einsum("gba,gbd->gad", tile_wide, picked, precision=lax.Precision.HIGHEST)
        else:
            products = jnp.einsum("gab,gbd->gad", tile_wide, picked, precision=lax.Precision.HIGHEST)
        onehot = (place_group[None, :] == targets[:, None]).astype(jnp.float32)
        return running + jnp.einsum("og,gad->oad", onehot, products, precision=lax.Precision.HIGHEST), None

    start_value = jnp.zeros((out_blocks, tile_size, feat_width), jnp.float32)
    running, _ = lax.scan(advance, start_value, (grouped, picks, places))
    return running


def reference(features, w_self, w_neigh, local_tiles, local_rows, local_cols, halo_tiles, halo_rows, halo_cols, cut_rows, cut_counts, cotangent):
    nodes_x = features.reshape(N_DOM, N_REP, R, D)
    cot_all = cotangent.reshape(N_DOM, N_REP, R, D)
    ltiles = local_tiles.reshape(N_DOM, N_REP, NL, TB, TB)
    lrows = local_rows.reshape(N_DOM, N_REP, NL)
    lcols = local_cols.reshape(N_DOM, N_REP, NL)
    htiles = halo_tiles.reshape(N_DOM, N_REP, NH, TB, TB)
    hrows = halo_rows.reshape(N_DOM, N_REP, NH)
    hcols = halo_cols.reshape(N_DOM, N_REP, NH)
    slot_index = jnp.arange(C, dtype=jnp.int32)
    live_slots = slot_index[None, None, None, :] < cut_counts[..., None]
    grad_scale = float(NODES) ** -0.5
    senders = jnp.arange(N_DOM, dtype=jnp.int32)

    def partition(carry, part_index):
        dx_halo, sum_self, sum_neigh = carry
        part_blocks = nodes_x[part_index].reshape(PB, TB, D)
        back_part = jnp.zeros((PB, TB, D), jnp.float32)
        out_rows = []
        rest_rows = []
        for rep_index in range(N_REP):
            cut_list = cut_rows[:, rep_index, part_index, :]
            gathered = jax.vmap(lambda block, idx: jnp.take(block, idx, axis=0))(nodes_x[:, rep_index], cut_list)
            live_here = live_slots[:, rep_index, part_index, :]
            incoming = jnp.where(live_here[:, :, None], gathered, jnp.zeros_like(gathered)).astype(jnp.bfloat16)
            halo_blocks = incoming.reshape(HB, TB, D)
            own_x = nodes_x[part_index, rep_index]
            summed = aggregate(part_blocks, ltiles[part_index, rep_index], lcols[part_index, rep_index], lrows[part_index, rep_index], RB, False)
            summed = summed + aggregate(halo_blocks, htiles[part_index, rep_index], hcols[part_index, rep_index], hrows[part_index, rep_index], RB, False)
            neighbour = summed.reshape(R, D).astype(jnp.bfloat16)
            preact = jnp.dot(own_x, w_self, preferred_element_type=jnp.float32) + jnp.dot(neighbour, w_neigh, preferred_element_type=jnp.float32)
            sigmoid_pre = jax.nn.sigmoid(preact)
            out_rows.append((preact * sigmoid_pre).astype(jnp.bfloat16))
            slope_value = sigmoid_pre * (1.0 + preact * (1.0 - sigmoid_pre))
            grad_pre = (cot_all[part_index, rep_index].astype(jnp.float32) * slope_value).astype(jnp.bfloat16)
            sum_self = sum_self + lax.dot_general(own_x, grad_pre, (((0,), (0,)), ((), ())), preferred_element_type=jnp.float32)
            sum_neigh = sum_neigh + lax.dot_general(neighbour, grad_pre, (((0,), (0,)), ((), ())), preferred_element_type=jnp.float32)
            grad_agg = jnp.dot(grad_pre, w_neigh.T, preferred_element_type=jnp.float32).astype(jnp.bfloat16)
            grad_self = jnp.dot(grad_pre, w_self.T, preferred_element_type=jnp.float32)
            agg_blocks = grad_agg.reshape(RB, TB, D)
            term = aggregate(agg_blocks, ltiles[part_index, rep_index], lrows[part_index, rep_index], lcols[part_index, rep_index], PB, True)
            back_part = back_part + lax.optimization_barrier(term.astype(jnp.bfloat16)).astype(jnp.float32)
            halo_back = aggregate(agg_blocks, htiles[part_index, rep_index], hrows[part_index, rep_index], hcols[part_index, rep_index], HB, True)
            halo_back = halo_back.astype(jnp.bfloat16).reshape(N_DOM, C, D).astype(jnp.float32)
            masked = jnp.where(live_here[:, :, None], halo_back, jnp.zeros_like(halo_back))
            dx_halo = dx_halo.at[senders[:, None], rep_index, cut_list].add(masked)
            rest_rows.append(grad_self)
        rest = jnp.stack(rest_rows) + back_part.reshape(N_REP, R, D)
        return (dx_halo, sum_self, sum_neigh), (jnp.stack(out_rows), rest)

    start_carry = (jnp.zeros((N_DOM, N_REP, R, D), jnp.float32), jnp.zeros((D, D), jnp.float32), jnp.zeros((D, D), jnp.float32))
    final_carry, stacked = lax.scan(partition, start_carry, jnp.arange(N_DOM, dtype=jnp.int32))
    dx_halo, sum_self, sum_neigh = final_carry
    out_all, rest_all = stacked
    out = out_all.reshape(NODES, D)
    d_x = (rest_all + dx_halo).astype(jnp.bfloat16).reshape(NODES, D)
    return out, d_x, sum_self * grad_scale, sum_neigh * grad_scale
```

```python
import functools

import jax
import jax.numpy as jnp
from jax import lax
from jax.experimental import pallas as pl
from jax.experimental.pallas import tpu as pltpu
from jax.sharding import PartitionSpec as P

VM = pl.BlockSpec(memory_space=pltpu.VMEM)
SM = pl.BlockSpec(memory_space=pltpu.SMEM)
TRANS_B = (((1,), (1,)), ((), ()))
TRANS_A = (((0,), (0,)), ((), ()))


def params(mib=60):
    return pltpu.CompilerParams(vmem_limit_bytes=mib * 2**20)


def sort_blocks(rows, cols, out_cols):
    count = rows.shape[0]
    ids = jnp.arange(count, dtype=jnp.int32)
    place = rows * out_cols + cols
    key = place * count + ids
    rank = jnp.sum((key[None, :] < key[:, None]).astype(jnp.int32), axis=1)
    hit = rank[None, :] == ids[:, None]
    order = jnp.sum(jnp.where(hit, ids[None, :], 0), axis=1)
    sorted_place = jnp.sum(jnp.where(hit, place[None, :], 0), axis=1)
    return jnp.stack([order, sorted_place])


def fill_dense(meta, tiles, dense, dense_t, zero_rows=256):
    size = tiles.shape[1]
    block_cols = dense.shape[1] // size
    for ref in (dense, dense_t):

        @pl.loop(0, ref.shape[0] // zero_rows)
        def _(i, ref=ref):
            ref[pl.ds(pl.multiple_of(i * zero_rows, zero_rows), zero_rows), :] = jnp.zeros(
                (zero_rows, ref.shape[1]), ref.dtype
            )

    def body(k, carry):
        total, before = carry
        place = meta[1, k]
        tile = tiles[meta[0, k]].astype(jnp.float32)
        total = jnp.where(place == before, total, 0.0) + tile
        row = pl.multiple_of((place // block_cols) * size, size)
        col = pl.multiple_of((place % block_cols) * size, size)
        dense[pl.ds(row, size), pl.ds(col, size)] = total.astype(dense.dtype)
        dense_t[pl.ds(col, size), pl.ds(row, size)] = total.T.astype(dense.dtype)
        return total, place

    lax.fori_loop(
        0, tiles.shape[0], body, (jnp.zeros((size, size), jnp.float32), jnp.int32(-1))
    )


def assemble_kernel(meta_l, meta_h, tiles_l, tiles_h, a_l, a_h, at_l, at_h):
    fill_dense(meta_l, tiles_l, a_l, at_l)
    fill_dense(meta_h, tiles_h, a_h, at_h)


def select_kernel(cuts, x, out, step=256):
    rows = x.shape[0]

    @pl.loop(0, out.shape[0] // step)
    def _(i):
        at = pl.ds(pl.multiple_of(i * step, step), step)
        ids = lax.broadcasted_iota(jnp.int32, (step, rows), 1)
        pick = (cuts[at, :] == ids).astype(jnp.float32).astype(jnp.bfloat16)
        out[at, :] = jnp.dot(pick, x[...], preferred_element_type=jnp.float32).astype(out.dtype)


def forward_kernel(a_l, a_h, part, halo, x, cot, w_self, w_neigh, out, neigh, grad, agg, step=256):
    @pl.loop(0, x.shape[0] // step)
    def _(i):
        at = pl.ds(pl.multiple_of(i * step, step), step)
        total = jnp.dot(a_l[at, :], part[...], preferred_element_type=jnp.float32)
        total += jnp.dot(a_h[at, :], halo[...], preferred_element_type=jnp.float32)
        near = total.astype(jnp.bfloat16)
        neigh[at, :] = near
        pre = jnp.dot(x[at, :], w_self[...], preferred_element_type=jnp.float32)
        pre += jnp.dot(near, w_neigh[...], preferred_element_type=jnp.float32)
        sig = jax.nn.sigmoid(pre)
        out[at, :] = (pre * sig).astype(out.dtype)
        slope = sig * (1.0 + pre * (1.0 - sig))
        g = (cot[at, :].astype(jnp.float32) * slope).astype(jnp.bfloat16)
        grad[at, :] = g
        agg[at, :] = lax.dot_general(
            g, w_neigh[...], TRANS_B, preferred_element_type=jnp.float32
        ).astype(agg.dtype)


def back_kernel(at_ref, agg, out, step=256):
    @pl.loop(0, out.shape[0] // step)
    def _(i):
        at = pl.ds(pl.multiple_of(i * step, step), step)
        out[at, :] = jnp.dot(at_ref[at, :], agg[...], preferred_element_type=jnp.float32).astype(out.dtype)


def weight_kernel(x, neigh, grad, d_self, d_neigh, scale=1.0, step=256):
    for left, result in ((x, d_self), (neigh, d_neigh)):
        for j in range(0, left.shape[1], step):
            result[j : j + step, :] = (
                lax.dot_general(left[:, j : j + step], grad[...], TRANS_A, preferred_element_type=jnp.float32)
                * scale
            )


def finish_kernel(cuts, back, part_back, grad, w_self, out, step=256):
    slots = back.shape[0]

    @pl.loop(0, out.shape[0] // step)
    def _(i):
        start = pl.multiple_of(i * step, step)
        at = pl.ds(start, step)
        ids = lax.broadcasted_iota(jnp.int32, (step, slots), 0) + start
        pick = (cuts[...] == ids).astype(jnp.float32).astype(jnp.bfloat16)
        total = jnp.dot(pick, back[...], preferred_element_type=jnp.float32)
        total += lax.dot_general(grad[at, :], w_self[...], TRANS_B, preferred_element_type=jnp.float32)
        out[at, :] = (total + part_back[at, :].astype(jnp.float32)).astype(out.dtype)


def shape(dims, dtype=jnp.bfloat16):
    return jax.ShapeDtypeStruct(dims, dtype)


def call(kernel, out_shape, specs, flops, moved, **kw):
    many = isinstance(out_shape, (tuple, list))
    return pl.pallas_call(
        kernel,
        out_shape=out_shape,
        in_specs=specs,
        out_specs=[VM] * len(out_shape) if many else VM,
        compiler_params=params(),
        cost_estimate=pl.CostEstimate(flops=flops, bytes_accessed=moved, transcendentals=0),
        **kw,
    )


def per_device(
    features, w_self, w_neigh, local_tiles, local_rows, local_cols, halo_tiles, halo_rows, halo_cols, cut_rows, cut_counts, cotangent
):
    rows, width = features.shape
    size = local_tiles.shape[1]
    reps = lax.axis_size("rep")
    doms = lax.axis_size("dom")
    part_rows = rows * reps
    slots = cut_rows.shape[3]
    halo_rows_n = slots * doms
    part = lax.all_gather(features, "rep", axis=0, tiled=True)
    live = jnp.arange(slots, dtype=jnp.int32)[None, :] < cut_counts[0, 0][:, None]
    cuts = jnp.where(live, cut_rows[0, 0], -1).reshape(-1)
    outgoing = call(select_kernel, shape((halo_rows_n, width)), [VM, VM], 2 * halo_rows_n * rows * width, 3 * 2**20)(
        cuts.reshape(-1, 1), features
    )
    halo = lax.all_to_all(outgoing.reshape(doms, slots, width), "dom", split_axis=0, concat_axis=0, tiled=True)
    halo = halo.reshape(halo_rows_n, width)
    meta_l = sort_blocks(local_rows, local_cols, part_rows // size)
    meta_h = sort_blocks(halo_rows, halo_cols, halo_rows_n // size)
    a_l, a_h, at_l, at_h = call(
        assemble_kernel,
        (shape((rows, part_rows)), shape((rows, halo_rows_n)), shape((part_rows, rows)), shape((halo_rows_n, rows))),
        [SM, SM, VM, VM],
        10**9,
        40 * 2**20,
    )(meta_l, meta_h, local_tiles, halo_tiles)
    rw = shape((rows, width))
    out, neigh, grad, agg = call(
        forward_kernel, (rw, rw, rw, rw), [VM] * 8, 2 * rows * width * (part_rows + halo_rows_n + 3 * width), 25 * 2**20
    )(a_l, a_h, part, halo, features, cotangent, w_self, w_neigh)
    term = call(back_kernel, shape((part_rows, width)), [VM, VM], 2 * rows * width * part_rows, 13 * 2**20)(at_l, agg)
    part_back = lax.psum_scatter(term, "rep", scatter_dimension=0, tiled=True)
    halo_back = call(back_kernel, shape((halo_rows_n, width)), [VM, VM], 2 * rows * width * halo_rows_n, 7 * 2**20)(
        at_h, agg
    )
    returned = lax.all_to_all(halo_back.reshape(doms, slots, width), "dom", split_axis=0, concat_axis=0, tiled=True)
    scale = float(rows * reps * doms) ** (-0.5)
    ww = shape((width, width), jnp.float32)
    part_self, part_neigh = call(
        functools.partial(weight_kernel, scale=scale), (ww, ww), [VM] * 3, 4 * rows * width * width, 5 * 2**20
    )(features, neigh, grad)
    both = jnp.concatenate([part_self, part_neigh], axis=1)
    both = lax.psum_scatter(both, "rep", scatter_dimension=0, tiled=True)
    both = lax.psum(both, "dom")
    d_x = call(finish_kernel, rw, [VM] * 5, 2 * rows * width * (halo_rows_n + width), 7 * 2**20)(
        cuts.reshape(1, -1), returned.reshape(halo_rows_n, width), part_back, grad, w_self
    )
    return out, d_x, both[:, :width], both[:, width:]


def solution(mesh):
    both = P(("dom", "rep"), None)
    in_specs = (
        both, P(), P(),
        P(("dom", "rep"), None, None), P(("dom", "rep")), P(("dom", "rep")),
        P(("dom", "rep"), None, None), P(("dom", "rep")), P(("dom", "rep")),
        P("dom", "rep", None, None), P("dom", "rep", None), both,
    )
    out_specs = (both, both, P("rep", None), P("rep", None))
    return jax.shard_map(per_device, mesh=mesh, in_specs=in_specs, out_specs=out_specs, check_vma=False)
```

```python
import functools

import jax
import jax.numpy as jnp
from jax import lax
from jax.experimental import pallas as pl
from jax.experimental.pallas import tpu as pltpu
from jax.sharding import PartitionSpec as P

F32, BF16 = jnp.float32, jnp.bfloat16
TRANS_B = (((1,), (1,)), ((), ()))
TRANS_A = (((0,), (0,)), ((), ()))
MESH = pl.DeviceIdType.MESH
CHUNK = 256


def dot(a, b, dims=None):
    if dims is None:
        return jnp.dot(a, b, preferred_element_type=F32)
    return lax.dot_general(a, b, dims, preferred_element_type=F32)


def span(start, size):
    return pl.ds(pl.multiple_of(start, size), size)


def running_sums(order, keep, tiles, hist, base, count):
    size = tiles.shape[1]
    unroll = 4

    def body(g, total):
        for u in range(unroll):
            k = g * unroll + u
            total = total * keep[base + k] + tiles[order[base + k]].astype(F32)
            hist[k] = total.astype(BF16)
        return total

    lax.fori_loop(0, count // unroll, body, jnp.zeros((size, size), F32))
    hist[count] = jnp.zeros((size, size), BF16)


def place_blocks(last, base, hist, dense):
    parts, rows, cols = dense.shape
    size = hist.shape[1]
    ri, cj = rows // size, cols // size

    def body(n, carry):
        c, i = n // ri, n % ri
        for j in range(cj):
            dense[c, span(i * size, size), j * size : (j + 1) * size] = hist[last[base + n * cj + j]]
        return carry

    lax.fori_loop(0, parts * ri, body, 0)


def layer_kernel(
    sizes,
    order, keep, last, cuts, x, cot, w_self, w_neigh, tiles_l_hbm, tiles_h_hbm,
    out, d_x, d_w,
    tiles_l, tiles_h, hist, a_l, a_h, outgoing, halo, part, total, neigh, grad, agg_t,
    t_far, t_right, t_left, ret, via, frm, w_send, w_recv, z_send, z_recv, fin,
    tile_sem, z_s, z_r, h_s, h_r, b_s, b_r, w_s, w_r, q_s, q_r, f_s, f_r,
):
    doms, reps, slots, scale = sizes
    rows, width = x.shape
    n_l, n_h = tiles_l.shape[0], tiles_h.shape[0]
    half, fhalf = rows // 2, width // 2
    chunks = rows // CHUNK
    q, r = lax.axis_index("dom"), lax.axis_index("rep")
    right, left = (r + 1) % reps, (r + reps - 1) % reps
    far = (r + 2) % reps

    load_l = pltpu.make_async_copy(tiles_l_hbm, tiles_l, tile_sem.at[0])
    load_h = pltpu.make_async_copy(tiles_h_hbm, tiles_h, tile_sem.at[1])
    load_l.start()
    load_h.start()

    barrier = pltpu.get_barrier_semaphore()

    @pl.loop(1, doms)
    def _(i):
        pl.semaphore_signal(barrier, inc=1, device_id={"dom": (q + i) % doms}, device_id_type=MESH)

    @pl.loop(1, reps)
    def _(i):
        pl.semaphore_signal(barrier, inc=1, device_id={"rep": (r + i) % reps}, device_id_type=MESH)

    halo[span(q * slots, slots), :] = jnp.zeros((slots, width), BF16)
    ret[span(q * slots, slots), :] = jnp.zeros((slots, width), BF16)
    pl.semaphore_wait(barrier, doms + reps - 2)

    def ring(src, dst, n, to):
        return pltpu.make_async_remote_copy(
            src_ref=src, dst_ref=dst, send_sem=z_s.at[n], recv_sem=z_r.at[n], device_id={"rep": to}, device_id_type=MESH
        )

    x0, x1 = x.at[pl.ds(0, half)], x.at[pl.ds(half, half)]
    z0 = ring(x0, part.at[0, pl.ds(0, half)], 0, right)
    z1 = ring(x1, part.at[1, pl.ds(half, half)], 1, left)
    z2 = ring(x1, part.at[0, pl.ds(half, half)], 2, right)
    z3 = ring(x0, part.at[1, pl.ds(0, half)], 3, left)
    for z in (z0, z1, z2, z3):
        z.start()

    def cross(src, dst, send, recv, peer, owner):
        return pltpu.make_async_remote_copy(
            src_ref=src, dst_ref=dst, send_sem=send.at[peer], recv_sem=recv.at[owner], device_id={"dom": peer}, device_id_type=MESH
        )

    def rows_of(ref, peer):
        return ref.at[span(peer * slots, slots)]

    def send_rows(src, dst, send, recv, first, count):
        for t in range(count):
            peer = first + t

            @pl.when(peer != q)
            def _(peer=peer):
                cross(rows_of(src, peer), rows_of(dst, q), send, recv, peer, q).start()

    def wait_rows(ref, send, recv, what):
        @pl.loop(1, doms)
        def _(i):
            peer = (q + i) % doms
            copy = cross(rows_of(ref, peer), rows_of(ref, peer), send, recv, peer, peer)
            copy.wait_recv() if what == "recv" else copy.wait_send()

    per = CHUNK // slots
    groups = doms // per

    @pl.loop(0, groups)
    def _(n):
        group = (q // per + 1 + n) % groups
        ids = jnp.broadcast_to(cuts[:, span(group * CHUNK, CHUNK)], (128, CHUNK)).T
        lane = lax.broadcasted_iota(jnp.int32, (CHUNK, 128), 1).astype(F32)
        pick = jnp.concatenate(
            [jnp.where(ids == lane + float(b * 128), 1.0, 0.0).astype(BF16) for b in range(rows // 128)], axis=1
        )
        outgoing[span(group * CHUNK, CHUNK), :] = dot(pick, x[...]).astype(BF16)
        send_rows(outgoing, halo, h_s, h_r, group * per, per)

    load_l.wait()
    running_sums(order, keep, tiles_l, hist, 0, n_l)
    z0.wait_recv()
    z4 = ring(part.at[0, pl.ds(0, half)], part.at[2, pl.ds(0, half)], 4, right)
    z4.start()
    z1.wait_recv()
    z5 = ring(part.at[1, pl.ds(half, half)], part.at[2, pl.ds(half, half)], 5, left)
    z5.start()
    place_blocks(last, 0, hist, a_l)

    @pl.loop(0, chunks)
    def _(i):
        at = span(i * CHUNK, CHUNK)
        total[at, :] = dot(a_l[r, at, :], x[...])

    load_h.wait()
    running_sums(order, keep, tiles_h, hist, n_l, n_h)
    place_blocks(last, a_l.shape[0] * a_l.shape[1] * a_l.shape[2] // (128 * 128), hist, a_h)
    z2.wait_recv()
    z3.wait_recv()

    @pl.loop(0, chunks)
    def _(i):
        at = span(i * CHUNK, CHUNK)
        total[at, :] += dot(a_l[left, at, :], part[0]) + dot(a_l[right, at, :], part[1])

    wait_rows(halo, h_s, h_r, "recv")

    @pl.loop(0, chunks)
    def _(i):
        at = span(i * CHUNK, CHUNK)
        hc = a_h.shape[2]
        acc = total[at, :]
        for c in range(a_h.shape[0]):
            acc += dot(a_h[c, at, :], halo[c * hc : (c + 1) * hc, :])
        total[at, :] = acc

    z4.wait_recv()
    z5.wait_recv()

    @pl.loop(0, chunks)
    def _(i):
        at = span(i * CHUNK, CHUNK)
        near = (total[at, :] + dot(a_l[far, at, :], part[2])).astype(BF16)
        neigh[at, :] = near
        pre = dot(x[at, :], w_self[...]) + dot(near, w_neigh[...])
        sig = jax.nn.sigmoid(pre)
        out[at, :] = (pre * sig).astype(BF16)
        slope = sig * (1.0 + pre * (1.0 - sig))
        g = (cot[at, :].astype(F32) * slope).astype(BF16)
        grad[at, :] = g
        agg_t[:, at] = dot(w_neigh[...], g, TRANS_B).astype(BF16)

    def term(ref, owner):
        @pl.loop(0, chunks)
        def _(i):
            at = span(i * CHUNK, CHUNK)
            ref[:, at] = dot(agg_t[...], a_l[owner, :, at]).astype(BF16)

    f0, f1 = pl.ds(0, fhalf), pl.ds(fhalf, fhalf)
    term(t_far, far)
    z6 = ring(t_far.at[f0], via.at[0], 6, right)
    z7 = ring(t_far.at[f1], via.at[1], 7, left)
    z6.start()
    z7.start()

    block = width // reps
    for m, lhs in enumerate((x, neigh)):
        for c in range(0, width, CHUNK):
            result = dot(lhs[:, c : c + CHUNK], grad[...], TRANS_A) * scale
            for k in range(CHUNK // block):
                at = (c // block + k) * 2 * block + m * block
                total[at : at + block, :] = result[k * block : (k + 1) * block, :]
    share = 2 * block // doms

    @pl.loop(0, doms)
    def _(n):
        peer = (q + 1 + n) % doms
        piece = [total[span(e * 2 * block + peer * share, share), :] for e in range(reps)]
        w_send[peer] = jnp.concatenate(piece, axis=0).astype(BF16)

        @pl.when(peer != q)
        def _():
            cross(w_send.at[peer], w_recv.at[q], w_s, w_r, peer, q).start()

    w_recv[q] = w_send[q]

    wait_rows(outgoing, h_s, h_r, "send")
    hc = a_h.shape[2]
    h_chunks = a_h.shape[0]

    @pl.loop(0, h_chunks)
    def _(n):
        c = (q // (hc // slots) + 1 + n) % h_chunks
        outgoing[span(c * hc, hc), :] = dot(agg_t[...], a_h[c]).T.astype(BF16)
        send_rows(outgoing, ret, b_s, b_r, c * (hc // slots), hc // slots)

    term(t_right, right)
    z8 = ring(t_right.at[f1], frm.at[0, f1], 8, right)
    z8.start()
    term(t_left, left)
    z9 = ring(t_left.at[f0], frm.at[1, f0], 9, left)
    z9.start()
    z6.wait_recv()
    t_right[f0, :] = (t_right[f0, :].astype(F32) + via[0].astype(F32)).astype(BF16)
    z10 = ring(t_right.at[f0], frm.at[0, f0], 10, right)
    z10.start()
    z7.wait_recv()
    t_left[f1, :] = (t_left[f1, :].astype(F32) + via[1].astype(F32)).astype(BF16)
    z11 = ring(t_left.at[f1], frm.at[1, f1], 11, left)
    z11.start()

    @pl.loop(0, chunks)
    def _(i):
        at = span(i * CHUNK, CHUNK)
        own = dot(agg_t[...], a_l[r, :, at])
        total[at, :] = own.T + dot(grad[at, :], w_self[...], TRANS_B)

    @pl.loop(1, doms)
    def _(i):
        peer = (q + i) % doms
        cross(w_recv.at[peer], w_recv.at[peer], w_s, w_r, peer, peer).wait_recv()

    summed = lax.fori_loop(
        0, doms, lambda p, acc: acc + w_recv[p].astype(F32), jnp.zeros(w_recv.shape[1:], F32)
    )
    for e in range(reps):
        z_send[e] = summed[e * share : (e + 1) * share, :]

    def small(peer, owner):
        return pltpu.make_async_remote_copy(
            src_ref=z_send.at[peer], dst_ref=z_recv.at[owner], send_sem=q_s.at[peer], recv_sem=q_r.at[owner],
            device_id={"rep": peer}, device_id_type=MESH,
        )

    @pl.loop(1, reps)
    def _(i):
        small((r + i) % reps, r).start()

    z_recv[r] = z_send[r]

    @pl.loop(1, reps)
    def _(i):
        peer = (r + i) % reps
        small(peer, peer).wait_recv()

    done = z_recv[0]
    for e in range(1, reps):
        done += z_recv[e]
    fin[q] = done

    @pl.loop(1, doms)
    def _(i):
        peer = (q + i) % doms
        cross(fin.at[q], fin.at[q], f_s, f_r, peer, q).start()

    wait_rows(ret, b_s, b_r, "recv")

    @pl.loop(0, chunks)
    def _(i):
        at = span(i * CHUNK, CHUNK)
        ids = lax.broadcasted_iota(jnp.int32, (CHUNK, ret.shape[0]), 0) + i * CHUNK
        pick = jnp.where(cuts[...] == ids.astype(F32), 1.0, 0.0).astype(BF16)
        total[at, :] += dot(pick, ret[...])

    for z in (z8, z9, z10, z11):
        z.wait_recv()

    @pl.loop(0, chunks)
    def _(i):
        at = span(i * CHUNK, CHUNK)
        other = frm[0, :, at].astype(F32) + frm[1, :, at].astype(F32)
        d_x[at, :] = (total[at, :] + other.T).astype(BF16)

    @pl.loop(1, doms)
    def _(i):
        peer = (q + i) % doms
        cross(fin.at[peer], fin.at[peer], f_s, f_r, peer, peer).wait_recv()

    @pl.loop(0, doms)
    def _(p):
        d_w[span(p * share, share), :] = fin[p]

    for z in (z0, z1, z2, z3, z4, z5, z6, z7, z8, z9, z10, z11):
        z.wait_send()
    wait_rows(outgoing, b_s, b_r, "send")

    @pl.loop(1, doms)
    def _(i):
        peer = (q + i) % doms
        cross(w_send.at[peer], w_recv.at[peer], w_s, w_r, peer, peer).wait_send()
        cross(fin.at[q], fin.at[q], f_s, f_r, peer, peer).wait_send()

    @pl.loop(1, reps)
    def _(i):
        peer = (r + i) % reps
        small(peer, peer).wait_send()


def sort_blocks(key, positions):
    count = key.shape[0]
    ids = jnp.arange(count, dtype=jnp.int32)
    before = ids[None, :] < ids[:, None]
    same = key[None, :] == key[:, None]
    rank = jnp.sum(((key[None, :] < key[:, None]) | (same & before)).astype(jnp.int32), axis=1)
    again = jnp.any(same & before, axis=1)
    hit = rank[None, :] == ids[:, None]
    order = jnp.sum(jnp.where(hit, ids[None, :], 0), axis=1)
    keep = jnp.sum(jnp.where(hit & again[None, :], 1.0, 0.0), axis=1)
    spots = jnp.arange(positions, dtype=jnp.int32)[:, None]
    upto = jnp.sum((key[None, :] <= spots).astype(jnp.int32), axis=1)
    full = jnp.any(key[None, :] == spots, axis=1)
    return order, keep, jnp.where(full, upto - 1, count)


def per_device(
    features, w_self, w_neigh, local_tiles, local_rows, local_cols, halo_tiles, halo_rows, halo_cols, cut_rows, cut_counts, cotangent
):
    rows, width = features.shape
    n_l, size, _ = local_tiles.shape
    n_h = halo_tiles.shape[0]
    reps, doms = lax.axis_size("rep"), lax.axis_size("dom")
    slots = cut_rows.shape[3]
    h_rows = slots * doms
    hc = min(512, h_rows)
    ri, cj, hj = rows // size, rows // size, hc // size
    key_l = ((local_cols // cj) * ri + local_rows) * cj + local_cols % cj
    key_h = ((halo_cols // hj) * ri + halo_rows) * hj + halo_cols % hj
    order_l, keep_l, last_l = sort_blocks(key_l, reps * ri * cj)
    order_h, keep_h, last_h = sort_blocks(key_h, ri * h_rows // size)
    order = jnp.concatenate([order_l, order_h])
    keep = jnp.concatenate([keep_l, keep_h])
    last = jnp.concatenate([last_l, last_h])
    live = jnp.arange(slots, dtype=jnp.int32)[None, :] < cut_counts[0, 0][:, None]
    cuts = jnp.where(live, cut_rows[0, 0], -1).astype(F32).reshape(1, -1)
    share = 2 * width // reps // doms
    scale = float(rows * reps * doms) ** (-0.5)
    vm, sm, hbm = (pl.BlockSpec(memory_space=m) for m in (pltpu.VMEM, pltpu.SMEM, pl.ANY))
    dma = lambda n: pltpu.SemaphoreType.DMA((n,))
    out, d_x, d_w = pl.pallas_call(
        functools.partial(layer_kernel, (doms, reps, slots, scale)),
        out_shape=(
            jax.ShapeDtypeStruct((rows, width), BF16),
            jax.ShapeDtypeStruct((rows, width), BF16),
            jax.ShapeDtypeStruct((2 * width // reps, width), F32),
        ),
        in_specs=[sm, sm, sm, vm, vm, vm, vm, vm, hbm, hbm],
        out_specs=[vm, vm, vm],
        scratch_shapes=[
            pltpu.VMEM((n_l, size, size), BF16),
            pltpu.VMEM((n_h, size, size), BF16),
            pltpu.VMEM((max(n_l, n_h) + 1, size, size), BF16),
            pltpu.VMEM((reps, rows, rows), BF16),
            pltpu.VMEM((h_rows // hc, rows, hc), BF16),
            pltpu.VMEM((h_rows, width), BF16),
            pltpu.VMEM((h_rows, width), BF16),
            pltpu.VMEM((3, rows, width), BF16),
            pltpu.VMEM((max(rows, 2 * width), width), F32),
            pltpu.VMEM((rows, width), BF16),
            pltpu.VMEM((rows, width), BF16),
            pltpu.VMEM((width, rows), BF16),
            pltpu.VMEM((width, rows), BF16),
            pltpu.VMEM((width, rows), BF16),
            pltpu.VMEM((width, rows), BF16),
            pltpu.VMEM((h_rows, width), BF16),
            pltpu.VMEM((2, width // 2, rows), BF16),
            pltpu.VMEM((2, width, rows), BF16),
            pltpu.VMEM((doms, reps * share, width), BF16),
            pltpu.VMEM((doms, reps * share, width), BF16),
            pltpu.VMEM((reps, share, width), F32),
            pltpu.VMEM((reps, share, width), F32),
            pltpu.VMEM((doms, share, width), F32),
            dma(2), dma(12), dma(12),
            dma(doms), dma(doms), dma(doms), dma(doms), dma(doms), dma(doms),
            dma(reps), dma(reps), dma(doms), dma(doms),
        ],
        compiler_params=pltpu.CompilerParams(
            collective_id=0, has_side_effects=True, vmem_limit_bytes=60 * 2**20
        ),
    )(order, keep, last, cuts, features, cotangent, w_self, w_neigh, local_tiles, halo_tiles)
    return out, d_x, d_w[: width // reps], d_w[width // reps :]


def solution(mesh):
    both = P(("dom", "rep"), None)
    in_specs = (
        both, P(), P(),
        P(("dom", "rep"), None, None), P(("dom", "rep")), P(("dom", "rep")),
        P(("dom", "rep"), None, None), P(("dom", "rep")), P(("dom", "rep")),
        P("dom", "rep", None, None), P("dom", "rep", None), both,
    )
    out_specs = (both, both, P("rep", None), P("rep", None))
    return jax.shard_map(per_device, mesh=mesh, in_specs=in_specs, out_specs=out_specs, check_vma=False)
```

```python
import functools
import math

import jax
import jax.numpy as jnp
from jax import lax
from jax.experimental import pallas as pl
from jax.experimental.pallas import tpu as pltpu
from jax.sharding import PartitionSpec as P

F32, BF16 = jnp.float32, jnp.bfloat16
TRANS_B = (((1,), (1,)), ((), ()))
TRANS_A = (((0,), (0,)), ((), ()))
MESH = pl.DeviceIdType.MESH
CHUNK = 256


def dot(a, b, dims=None):
    if dims is None:
        return jnp.dot(a, b, preferred_element_type=F32)
    return lax.dot_general(a, b, dims, preferred_element_type=F32)


def span(start, size):
    return pl.ds(pl.multiple_of(start, size), size)


def running_sums(order, keep, tiles, hist, base, count):
    size = tiles.shape[1]
    unroll = 4

    def body(g, total):
        for u in range(unroll):
            k = g * unroll + u
            total = total * keep[0, base + k] + tiles[order[0, base + k]].astype(F32)
            hist[k] = total.astype(BF16)
        return total

    lax.fori_loop(0, count // unroll, body, jnp.zeros((size, size), F32))
    hist[count] = jnp.zeros((size, size), BF16)


def place_blocks(last, base, hist, dense):
    parts, rows, cols = dense.shape
    size = hist.shape[1]
    ri, cj = rows // size, cols // size

    def body(n, carry):
        c, i = n // ri, n % ri
        for j in range(cj):
            dense[c, span(i * size, size), j * size : (j + 1) * size] = hist[last[0, base + n * cj + j]]
        return carry

    lax.fori_loop(0, parts * ri, body, 0)


def layer_kernel(
    sizes,
    order, keep, last, cuts, x, cot, w_self, w_neigh, tiles_l_hbm, tiles_h_hbm,
    out, d_x, d_w,
    tiles_l, tiles_h, hist, a_l, a_h, outgoing, halo, part, total, neigh, grad, agg_t,
    t_far, t_right, t_left, ret, via, frm, w_pair, w_send, w_recv, z_send, z_recv, fin, pass_h, pass_b,
    tile_sem, z_s, z_r, h_s, h_r, b_s, b_r, w_s, w_r, q_s, q_r, f_s, f_r, p_s, p_r, hp_s, hp_r, bp_s, bp_r,
):
    doms, reps, slots, scale = sizes
    rows, width = x.shape
    n_l, n_h = tiles_l.shape[0], tiles_h.shape[0]
    hist_base = order.shape[1] // 2
    half, fhalf = rows // 2, width // 2
    chunks = rows // CHUNK
    q, r = lax.axis_index("dom"), lax.axis_index("rep")
    right, left = (r + 1) % reps, (r + reps - 1) % reps
    far = (r + 2) % reps
    chips = doms // 2
    side = math.isqrt(chips)
    chip, core = q // 2, q % 2
    cx, cy = chip // side, chip % side
    twin = chip * 2 + 1 - core

    def at_chip(ax, ay, c):
        return ((ax + side) % side * side + (ay + side) % side) * 2 + c

    load_l = pltpu.make_async_copy(tiles_l_hbm, tiles_l, tile_sem.at[0])
    load_h = pltpu.make_async_copy(tiles_h_hbm, tiles_h, tile_sem.at[1])
    load_l.start()
    load_h.start()

    barrier = pltpu.get_barrier_semaphore()

    @pl.loop(1, doms)
    def _(i):
        pl.semaphore_signal(barrier, inc=1, device_id={"dom": (q + i) % doms}, device_id_type=MESH)

    @pl.loop(1, reps)
    def _(i):
        pl.semaphore_signal(barrier, inc=1, device_id={"rep": (r + i) % reps}, device_id_type=MESH)

    halo[span(q * slots, slots), :] = jnp.zeros((slots, width), BF16)
    ret[span(q * slots, slots), :] = jnp.zeros((slots, width), BF16)
    pl.semaphore_wait(barrier, doms + reps - 2)

    def ring(src, dst, n, to):
        return pltpu.make_async_remote_copy(
            src_ref=src, dst_ref=dst, send_sem=z_s.at[n], recv_sem=z_r.at[n], device_id={"rep": to}, device_id_type=MESH
        )

    x0, x1 = x.at[pl.ds(0, half)], x.at[pl.ds(half, half)]
    z0 = ring(x0, part.at[0, pl.ds(0, half)], 0, right)
    z1 = ring(x1, part.at[1, pl.ds(half, half)], 1, left)
    z2 = ring(x1, part.at[0, pl.ds(half, half)], 2, right)
    z3 = ring(x0, part.at[1, pl.ds(0, half)], 3, left)
    for z in (z0, z1, z2, z3):
        z.start()

    def cross(src, dst, send, recv, peer, owner):
        return pltpu.make_async_remote_copy(
            src_ref=src, dst_ref=dst, send_sem=send.at[peer], recv_sem=recv.at[owner], device_id={"dom": peer}, device_id_type=MESH
        )

    def cross_to(src, dst, send, recv, peer):
        return pltpu.make_async_remote_copy(
            src_ref=src, dst_ref=dst, send_sem=send, recv_sem=recv, device_id={"dom": peer}, device_id_type=MESH
        )

    def rows_of(ref, peer):
        return ref.at[span(peer * slots, slots)]

    def send_rows(src, dst, passed, send, recv, pass_recv, first, count):
        for t in range(count):
            peer = first + t
            dx, dy = (peer // 2 // side - cx + side) % side, (peer // 2 % side - cy + side) % side
            detour = (dx % 2 + dy % 2 == 0) & (dx + dy > 0) if side == 4 else None

            def direct(peer=peer):
                cross(rows_of(src, peer), rows_of(dst, q), send, recv, peer, q).start()

            if detour is None:
                pl.when(peer != q)(direct)
                continue
            pl.when((peer != q) & jnp.logical_not(detour))(direct)

            @pl.when(detour)
            def _(peer=peer, dx=dx, dy=dy):
                slot = (dx // 2 + dy // 2 * 2 - 1) * 2 + peer % 2
                pltpu.make_async_remote_copy(
                    src_ref=rows_of(src, peer), dst_ref=passed.at[slot], send_sem=send.at[peer], recv_sem=pass_recv.at[slot],
                    device_id={"dom": at_chip(cx - dx // 2, cy - dy // 2, core)}, device_id_type=MESH,
                ).start()

    def pass_on(dst, passed, send, recv, pass_recv, start):
        if side != 4:
            return

        @pl.loop(0, 6)
        def _(slot):
            kx, ky = (slot // 2 + 1) % 2, (slot // 2 + 1) // 2
            owner = at_chip(cx + kx, cy + ky, core)
            copy = pltpu.make_async_remote_copy(
                src_ref=passed.at[slot], dst_ref=rows_of(dst, owner), send_sem=send.at[slot], recv_sem=recv.at[owner],
                device_id={"dom": at_chip(cx - kx, cy - ky, slot % 2)}, device_id_type=MESH,
            )
            if start:
                pltpu.make_async_remote_copy(
                    src_ref=passed.at[slot], dst_ref=passed.at[slot], send_sem=send.at[slot], recv_sem=pass_recv.at[slot],
                    device_id={"dom": owner}, device_id_type=MESH,
                ).wait_recv()
                copy.start()
            else:
                copy.wait_send()

    def wait_rows(ref, send, recv, what):
        @pl.loop(1, doms)
        def _(i):
            peer = (q + i) % doms
            copy = cross(rows_of(ref, peer), rows_of(ref, peer), send, recv, peer, peer)
            copy.wait_recv() if what == "recv" else copy.wait_send()

    per = CHUNK // slots
    groups = doms // per

    @pl.loop(0, groups)
    def _(n):
        if side == 4:
            step = sum(jnp.where(n == k, v, 0) for k, v in enumerate((5, 4, 1, 3, 2, 7, 6, 0)))
            group = (cx + step // 2) % side * 2 + (cy // 2 + step % 2) % 2
        else:
            group = (q // per + 1 + n) % groups
        lane = lax.broadcasted_iota(jnp.int32, (CHUNK, 128), 1).astype(F32)
        ids = jnp.concatenate(
            [jnp.broadcast_to(cuts[pl.ds(group * (CHUNK // 128) + b, 1), :], (128, 128)).T for b in range(CHUNK // 128)], axis=0
        )
        pick = jnp.concatenate(
            [jnp.where(ids == lane + float(b * 128), 1.0, 0.0).astype(BF16) for b in range(rows // 128)], axis=1
        )
        outgoing[span(group * CHUNK, CHUNK), :] = dot(pick, x[...]).astype(BF16)
        send_rows(outgoing, halo, pass_h, h_s, h_r, hp_r, group * per, per)

    load_l.wait()
    running_sums(order, keep, tiles_l, hist, 0, n_l)
    pass_on(halo, pass_h, hp_s, h_r, hp_r, True)
    z0.wait_recv()
    z4 = ring(part.at[0, pl.ds(0, half)], part.at[2, pl.ds(0, half)], 4, right)
    z4.start()
    z1.wait_recv()
    z5 = ring(part.at[1, pl.ds(half, half)], part.at[2, pl.ds(half, half)], 5, left)
    z5.start()
    place_blocks(last, 0, hist, a_l)

    @pl.loop(0, chunks)
    def _(i):
        at = span(i * CHUNK, CHUNK)
        total[at, :] = dot(a_l[r, at, :], x[...])

    load_h.wait()
    running_sums(order, keep, tiles_h, hist, hist_base, n_h)
    place_blocks(last, a_l.shape[0] * a_l.shape[1] * a_l.shape[2] // (128 * 128), hist, a_h)
    z2.wait_recv()
    z3.wait_recv()

    @pl.loop(0, chunks)
    def _(i):
        at = span(i * CHUNK, CHUNK)
        total[at, :] += dot(a_l[left, at, :], part[0]) + dot(a_l[right, at, :], part[1])

    wait_rows(halo, h_s, h_r, "recv")

    @pl.loop(0, chunks)
    def _(i):
        at = span(i * CHUNK, CHUNK)
        hc = a_h.shape[2]
        acc = total[at, :]
        for c in range(a_h.shape[0]):
            acc += dot(a_h[c, at, :], halo[c * hc : (c + 1) * hc, :])
        total[at, :] = acc

    z4.wait_recv()
    z5.wait_recv()

    @pl.loop(0, chunks)
    def _(i):
        at = span(i * CHUNK, CHUNK)
        near = (total[at, :] + dot(a_l[far, at, :], part[2])).astype(BF16)
        neigh[at, :] = near
        pre = dot(x[at, :], w_self[...]) + dot(near, w_neigh[...])
        sig = jax.nn.sigmoid(pre)
        out[at, :] = (pre * sig).astype(BF16)
        slope = sig * (1.0 + pre * (1.0 - sig))
        g = (cot[at, :].astype(F32) * slope).astype(BF16)
        grad[at, :] = g
        agg_t[:, at] = dot(w_neigh[...], g, TRANS_B).astype(BF16)

    def term(ref, owner):
        @pl.loop(0, chunks)
        def _(i):
            at = span(i * CHUNK, CHUNK)
            ref[:, at] = dot(agg_t[...], a_l[owner, :, at]).astype(BF16)

    f0, f1 = pl.ds(0, fhalf), pl.ds(fhalf, fhalf)
    term(t_far, far)
    z6 = ring(t_far.at[f0], via.at[0], 6, right)
    z7 = ring(t_far.at[f1], via.at[1], 7, left)
    z6.start()
    z7.start()

    block = width // reps
    for m, lhs in enumerate((x, neigh)):
        for c in range(0, width, CHUNK):
            result = dot(lhs[:, c : c + CHUNK], grad[...], TRANS_A) * scale
            for k in range(CHUNK // block):
                at = (c // block + k) * 2 * block + m * block
                total[at : at + block, :] = result[k * block : (k + 1) * block, :]
    share = 2 * block // doms

    def slices(peer):
        return jnp.concatenate([total[span(e * 2 * block + peer * share, share), :] for e in range(reps)], axis=0)

    @pl.loop(0, chips)
    def _(n):
        w_pair[0, n] = slices(n * 2 + 1 - core).astype(BF16)

    pair = cross_to(w_pair.at[0], w_pair.at[1], p_s.at[0], p_r.at[0], twin)
    pair.start()

    wait_rows(outgoing, h_s, h_r, "send")
    hc = a_h.shape[2]
    h_chunks = a_h.shape[0]

    @pl.loop(0, h_chunks)
    def _(n):
        if side == 4:
            c = (cx + sum(jnp.where(n == k, v, 0) for k, v in enumerate((2, 0, 1, 3)))) % side
        else:
            c = (q // (hc // slots) + 1 + n) % h_chunks
        outgoing[span(c * hc, hc), :] = dot(agg_t[...], a_h[c]).T.astype(BF16)
        send_rows(outgoing, ret, pass_b, b_s, b_r, bp_r, c * (hc // slots), hc // slots)

    pair.wait_recv()

    def same_core(i):
        return (chip + i) % chips

    def slice_to(peer, owner):
        return cross_to(w_send.at[peer], w_recv.at[owner], w_s.at[peer], w_r.at[owner], peer * 2 + core)

    @pl.loop(0, chips)
    def _(n):
        peer = same_core(n + 1)
        w_send[peer] = (slices(peer * 2 + core) + w_pair[1, peer].astype(F32)).astype(BF16)

        @pl.when(peer != chip)
        def _():
            slice_to(peer, chip).start()

    w_recv[chip] = w_send[chip]

    term(t_right, right)
    z8 = ring(t_right.at[f1], frm.at[0, f1], 8, right)
    z8.start()
    term(t_left, left)
    z9 = ring(t_left.at[f0], frm.at[1, f0], 9, left)
    z9.start()
    z6.wait_recv()
    t_right[f0, :] = (t_right[f0, :].astype(F32) + via[0].astype(F32)).astype(BF16)
    z10 = ring(t_right.at[f0], frm.at[0, f0], 10, right)
    z10.start()
    z7.wait_recv()
    t_left[f1, :] = (t_left[f1, :].astype(F32) + via[1].astype(F32)).astype(BF16)
    z11 = ring(t_left.at[f1], frm.at[1, f1], 11, left)
    z11.start()
    pass_on(ret, pass_b, bp_s, b_r, bp_r, True)

    @pl.loop(0, chunks)
    def _(i):
        at = span(i * CHUNK, CHUNK)
        own = dot(agg_t[...], a_l[r, :, at])
        total[at, :] = own.T + dot(grad[at, :], w_self[...], TRANS_B)

    @pl.loop(1, chips)
    def _(i):
        slice_to(same_core(i), same_core(i)).wait_recv()

    summed = lax.fori_loop(
        0, chips, lambda p, acc: acc + w_recv[p].astype(F32), jnp.zeros(w_recv.shape[1:], F32)
    )
    for e in range(reps):
        z_send[e] = summed[e * share : (e + 1) * share, :]

    def small(peer, owner):
        return pltpu.make_async_remote_copy(
            src_ref=z_send.at[peer], dst_ref=z_recv.at[owner], send_sem=q_s.at[peer], recv_sem=q_r.at[owner],
            device_id={"rep": peer}, device_id_type=MESH,
        )

    @pl.loop(1, reps)
    def _(i):
        small((r + i) % reps, r).start()

    z_recv[r] = z_send[r]

    @pl.loop(1, reps)
    def _(i):
        peer = (r + i) % reps
        small(peer, peer).wait_recv()

    done = z_recv[0]
    for e in range(1, reps):
        done += z_recv[e]
    fin[core, chip] = done

    def final_to(peer, owner):
        return cross_to(fin.at[core, owner], fin.at[core, owner], f_s.at[peer], f_r.at[owner], peer * 2 + core)

    @pl.loop(1, chips)
    def _(i):
        final_to(same_core(i), chip).start()

    wait_rows(ret, b_s, b_r, "recv")

    @pl.loop(0, chunks)
    def _(i):
        at = span(i * CHUNK, CHUNK)
        ids = (lax.broadcasted_iota(jnp.int32, (CHUNK, 128), 0) + i * CHUNK).astype(F32)
        pick = jnp.concatenate(
            [jnp.where(cuts[b : b + 1, :] == ids, 1.0, 0.0).astype(BF16) for b in range(ret.shape[0] // 128)], axis=1
        )
        total[at, :] += dot(pick, ret[...])

    @pl.loop(1, chips)
    def _(i):
        final_to(same_core(i), same_core(i)).wait_recv()

    to_twin = cross_to(fin.at[core], fin.at[core], p_s.at[1], p_r.at[1], twin)
    to_twin.start()
    for z in (z8, z9, z10, z11):
        z.wait_recv()

    @pl.loop(0, chunks)
    def _(i):
        at = span(i * CHUNK, CHUNK)
        other = frm[0, :, at].astype(F32) + frm[1, :, at].astype(F32)
        d_x[at, :] = (total[at, :] + other.T).astype(BF16)

    cross_to(fin.at[1 - core], fin.at[1 - core], p_s.at[1], p_r.at[1], twin).wait_recv()

    @pl.loop(0, chips)
    def _(p):
        for c in range(2):
            d_w[span((p * 2 + c) * share, share), :] = fin[c, p]

    for z in (z0, z1, z2, z3, z4, z5, z6, z7, z8, z9, z10, z11):
        z.wait_send()
    wait_rows(outgoing, b_s, b_r, "send")

    pass_on(halo, pass_h, hp_s, h_r, hp_r, False)
    pass_on(ret, pass_b, bp_s, b_r, bp_r, False)
    pair.wait_send()
    to_twin.wait_send()

    @pl.loop(1, chips)
    def _(i):
        slice_to(same_core(i), same_core(i)).wait_send()
        final_to(same_core(i), chip).wait_send()

    @pl.loop(1, reps)
    def _(i):
        peer = (r + i) % reps
        small(peer, peer).wait_send()


def index_kernel(sizes, lr, lc, hr, hk, cut_rows, cut_counts, order, keep, last, cuts, pad, wide):
    ri, cj, hj, n_pos = sizes
    n = pad.shape[1]

    def spread(row):
        return jnp.broadcast_to(row, (n, n))

    i = lax.broadcasted_iota(jnp.int32, (n, n), 0)
    j = lax.broadcasted_iota(jnp.int32, (n, n), 1)
    base = 0
    for m, (row, col, per) in enumerate(((lr, lc, cj), (hr, hk, hj))):
        count = row.shape[1]
        pad[...] = jnp.full(pad.shape, 1e6, F32)
        key = ((col[...] // per) * ri + row[...]) * per + col[...] % per
        pad[0:1, 0:count] = key.astype(F32)
        across = spread(pad[0:1, :])
        down = across.T
        same = across == down
        rank = jnp.sum(jnp.where((across < down) | (same & (j < i)), 1.0, 0.0), axis=1, keepdims=True)
        again = jnp.max(jnp.where(same & (j < i), 1.0, 0.0), axis=1, keepdims=True)
        hit = jnp.where(rank == j.astype(F32), 1.0, 0.0)
        order[0:1, m * n : (m + 1) * n] = jnp.sum(hit * i.astype(F32), axis=0, keepdims=True).astype(jnp.int32)
        keep[0:1, m * n : (m + 1) * n] = jnp.sum(hit * again, axis=0, keepdims=True)
        for p in range(0, n_pos[m], n):
            spot = j.astype(F32) + float(p)
            upto = jnp.sum(jnp.where(down <= spot, 1.0, 0.0), axis=0, keepdims=True)
            full = jnp.max(jnp.where(down == spot, 1.0, 0.0), axis=0, keepdims=True)
            found = jnp.where(full > 0.0, upto - 1.0, float(count)).astype(jnp.int32)
            width = min(n, n_pos[m] - p)
            last[0:1, base + p : base + p + width] = found[:, :width]
        base += n_pos[m]
    groups, slots = cut_rows.shape
    pad[...] = jnp.zeros(pad.shape, F32)
    pad[0:1, 0:groups] = cut_counts[...].astype(F32)
    live = j[:groups, :slots].astype(F32) < spread(pad[0:1, :]).T[:groups, :slots]
    wide[:, 0:slots] = jnp.where(live, cut_rows[...].astype(F32), -1.0)
    even = wide[pl.ds(0, groups // 2, stride=2), :]
    odd = wide[pl.ds(1, groups // 2, stride=2), :]
    lane = lax.broadcasted_iota(jnp.int32, even.shape, 1)
    cuts[...] = jnp.where(lane < slots, even, pltpu.roll(odd, slots, 1))


def deliver_kernel(out, d_x, d_w, out_to, d_x_to, d_self, d_neigh, big, small, sem_in, sem_out):
    rows, half = d_self.shape[0], out.shape[0] // 2
    steps = []
    for m, (a, b) in enumerate(((out, out_to), (d_x, d_x_to))):
        for k in range(2):
            at = pl.ds(k * half, half)
            steps.append((a.at[at], big.at[m, at], b.at[at]))
    for m, b in enumerate((d_self, d_neigh)):
        steps.append((d_w.at[pl.ds(m * rows, rows)], small.at[m], b))
    loads = [pltpu.make_async_copy(a, v, sem_in.at[k]) for k, (a, v, _) in enumerate(steps)]
    stores = [pltpu.make_async_copy(v, b, sem_out.at[k]) for k, (_, v, b) in enumerate(steps)]
    for c in loads:
        c.start()
    for c, d in zip(loads, stores):
        c.wait()
        d.start()
    for d in stores:
        d.wait()


def per_device(
    features, w_self, w_neigh, local_tiles, local_rows, local_cols, halo_tiles, halo_rows, halo_cols, cut_rows, cut_counts, cotangent
):
    rows, width = features.shape
    n_l, size, _ = local_tiles.shape
    n_h = halo_tiles.shape[0]
    reps, doms = lax.axis_size("rep"), lax.axis_size("dom")
    slots = cut_rows.shape[3]
    h_rows = slots * doms
    hc = min(512, h_rows)
    ri, cj, hj = rows // size, rows // size, hc // size
    vm, sm, hbm = (pl.BlockSpec(memory_space=m) for m in (pltpu.VMEM, pltpu.SMEM, pl.ANY))
    n = 128
    n_pos = (reps * ri * cj, ri * h_rows // size)
    order, keep, last, cuts = pl.pallas_call(
        functools.partial(index_kernel, (ri, cj, hj, n_pos)),
        out_shape=(
            jax.ShapeDtypeStruct((1, 2 * n), jnp.int32),
            jax.ShapeDtypeStruct((1, 2 * n), F32),
            jax.ShapeDtypeStruct((1, sum(n_pos)), jnp.int32),
            jax.ShapeDtypeStruct((h_rows // n, n), F32),
        ),
        in_specs=[vm] * 6,
        out_specs=[vm] * 4,
        scratch_shapes=[pltpu.VMEM((8, n), F32), pltpu.VMEM((doms, n), F32)],
    )(
        local_rows.reshape(1, -1), local_cols.reshape(1, -1), halo_rows.reshape(1, -1), halo_cols.reshape(1, -1),
        cut_rows[0, 0], cut_counts[0],
    )
    share = 2 * width // reps // doms
    scale = float(rows * reps * doms) ** (-0.5)
    chips = doms // 2
    dma = lambda n: pltpu.SemaphoreType.DMA((n,))
    out, d_x, d_w = pl.pallas_call(
        functools.partial(layer_kernel, (doms, reps, slots, scale)),
        out_shape=(
            jax.ShapeDtypeStruct((rows, width), BF16),
            jax.ShapeDtypeStruct((rows, width), BF16),
            jax.ShapeDtypeStruct((2 * width // reps, width), F32),
        ),
        in_specs=[sm, sm, sm, vm, vm, vm, vm, vm, hbm, hbm],
        out_specs=[vm, vm, vm],
        scratch_shapes=[
            pltpu.VMEM((n_l, size, size), BF16),
            pltpu.VMEM((n_h, size, size), BF16),
            pltpu.VMEM((max(n_l, n_h) + 1, size, size), BF16),
            pltpu.VMEM((reps, rows, rows), BF16),
            pltpu.VMEM((h_rows // hc, rows, hc), BF16),
            pltpu.VMEM((h_rows, width), BF16),
            pltpu.VMEM((h_rows, width), BF16),
            pltpu.VMEM((3, rows, width), BF16),
            pltpu.VMEM((max(rows, 2 * width), width), F32),
            pltpu.VMEM((rows, width), BF16),
            pltpu.VMEM((rows, width), BF16),
            pltpu.VMEM((width, rows), BF16),
            pltpu.VMEM((width, rows), BF16),
            pltpu.VMEM((width, rows), BF16),
            pltpu.VMEM((width, rows), BF16),
            pltpu.VMEM((h_rows, width), BF16),
            pltpu.VMEM((2, width // 2, rows), BF16),
            pltpu.VMEM((2, width, rows), BF16),
            pltpu.VMEM((2, chips, reps * share, width), BF16),
            pltpu.VMEM((chips, reps * share, width), BF16),
            pltpu.VMEM((chips, reps * share, width), BF16),
            pltpu.VMEM((reps, share, width), F32),
            pltpu.VMEM((reps, share, width), F32),
            pltpu.VMEM((2, chips, share, width), F32),
            pltpu.VMEM((6, slots, width), BF16),
            pltpu.VMEM((6, slots, width), BF16),
            dma(2), dma(12), dma(12),
            dma(doms), dma(doms), dma(doms), dma(doms), dma(chips), dma(chips),
            dma(reps), dma(reps), dma(chips), dma(chips), dma(2), dma(2), dma(6), dma(6), dma(6), dma(6),
        ],
        compiler_params=pltpu.CompilerParams(
            collective_id=0, has_side_effects=True, vmem_limit_bytes=60 * 2**20
        ),
    )(order, keep, last, cuts, features, cotangent, w_self, w_neigh, local_tiles, halo_tiles)
    part_w = jax.ShapeDtypeStruct((width // reps, width), F32)
    return pl.pallas_call(
        deliver_kernel,
        out_shape=(
            jax.ShapeDtypeStruct((rows, width), BF16), jax.ShapeDtypeStruct((rows, width), BF16), part_w, part_w,
        ),
        in_specs=[hbm] * 3,
        out_specs=[hbm] * 4,
        scratch_shapes=[
            pltpu.VMEM((2, rows, width), BF16), pltpu.VMEM((2, width // reps, width), F32), dma(6), dma(6),
        ],
    )(out, d_x, d_w)


def solution(mesh):
    both = P(("dom", "rep"), None)
    in_specs = (
        both, P(), P(),
        P(("dom", "rep"), None, None), P(("dom", "rep")), P(("dom", "rep")),
        P(("dom", "rep"), None, None), P(("dom", "rep")), P(("dom", "rep")),
        P("dom", "rep", None, None), P("dom", "rep", None), both,
    )
    out_specs = (both, both, P("rep", None), P("rep", None))
    return jax.shard_map(per_device, mesh=mesh, in_specs=in_specs, out_specs=out_specs, check_vma=False)
```

```python
import functools
import math

import jax
import jax.numpy as jnp
from jax import lax
from jax.experimental import pallas as pl
from jax.experimental.pallas import tpu as pltpu
from jax.sharding import PartitionSpec as P

F32, BF16 = jnp.float32, jnp.bfloat16
TRANS_B = (((1,), (1,)), ((), ()))
TRANS_A = (((0,), (0,)), ((), ()))
MESH = pl.DeviceIdType.MESH
CHUNK = 256


def dot(a, b, dims=None):
    if dims is None:
        return jnp.dot(a, b, preferred_element_type=F32)
    return lax.dot_general(a, b, dims, preferred_element_type=F32)


def span(start, size):
    return pl.ds(pl.multiple_of(start, size), size)


def running_sums(order, keep, tiles, hist, base, count):
    size = tiles.shape[1]
    unroll = 4

    def body(g, total):
        for u in range(unroll):
            k = g * unroll + u
            total = total * keep[0, base + k] + tiles[order[0, base + k]].astype(F32)
            hist[k] = total.astype(BF16)
        return total

    lax.fori_loop(0, count // unroll, body, jnp.zeros((size, size), F32))
    hist[count] = jnp.zeros((size, size), BF16)


def place_blocks(last, base, hist, dense):
    parts, rows, cols = dense.shape
    size = hist.shape[1]
    ri, cj = rows // size, cols // size

    def body(n, carry):
        c, i = n // ri, n % ri
        for j in range(cj):
            dense[c, span(i * size, size), j * size : (j + 1) * size] = hist[last[0, base + n * cj + j]]
        return carry

    lax.fori_loop(0, parts * ri, body, 0)


def layer_kernel(
    sizes,
    order, keep, last, cuts, x, cot, w_self, w_neigh, tiles_l_hbm, tiles_h_hbm,
    out, d_x, d_w,
    tiles_l, tiles_h, hist, a_l, a_h, outgoing, halo, part, total, pre_self, neigh, grad, agg_t,
    t_far, t_right, t_left, ret, via, frm, w_pair, w_send, w_recv, z_send, z_recv, fin, pass_h, pass_b,
    tile_sem, z_s, z_r, h_s, h_r, b_s, b_r, w_s, w_r, q_s, q_r, f_s, f_r, p_s, p_r, hp_s, hp_r, bp_s, bp_r,
):
    doms, reps, slots, scale = sizes
    rows, width = x.shape
    n_l, n_h = tiles_l.shape[0], tiles_h.shape[0]
    hist_base = order.shape[1] // 2
    half, fhalf = rows // 2, width // 2
    chunks = rows // CHUNK
    q, r = lax.axis_index("dom"), lax.axis_index("rep")
    right, left = (r + 1) % reps, (r + reps - 1) % reps
    far = (r + 2) % reps
    chips = doms // 2
    side = math.isqrt(chips)
    chip, core = q // 2, q % 2
    cx, cy = chip // side, chip % side
    twin = chip * 2 + 1 - core

    def at_chip(ax, ay, c):
        return ((ax + side) % side * side + (ay + side) % side) * 2 + c

    load_l = pltpu.make_async_copy(tiles_l_hbm, tiles_l, tile_sem.at[0])
    load_h = pltpu.make_async_copy(tiles_h_hbm, tiles_h, tile_sem.at[1])
    load_l.start()
    load_h.start()

    barrier = pltpu.get_barrier_semaphore()

    @pl.loop(1, doms)
    def _(i):
        pl.semaphore_signal(barrier, inc=1, device_id={"dom": (q + i) % doms}, device_id_type=MESH)

    @pl.loop(1, reps)
    def _(i):
        pl.semaphore_signal(barrier, inc=1, device_id={"rep": (r + i) % reps}, device_id_type=MESH)

    halo[span(q * slots, slots), :] = jnp.zeros((slots, width), BF16)
    ret[span(q * slots, slots), :] = jnp.zeros((slots, width), BF16)
    pl.semaphore_wait(barrier, doms + reps - 2)

    def ring(src, dst, n, to):
        return pltpu.make_async_remote_copy(
            src_ref=src, dst_ref=dst, send_sem=z_s.at[n], recv_sem=z_r.at[n], device_id={"rep": to}, device_id_type=MESH
        )

    x0, x1 = x.at[pl.ds(0, half)], x.at[pl.ds(half, half)]
    z0 = ring(x0, part.at[0, pl.ds(0, half)], 0, right)
    z1 = ring(x1, part.at[1, pl.ds(half, half)], 1, left)
    z2 = ring(x1, part.at[0, pl.ds(half, half)], 2, right)
    z3 = ring(x0, part.at[1, pl.ds(0, half)], 3, left)
    for z in (z0, z1, z2, z3):
        z.start()

    def cross(src, dst, send, recv, peer, owner):
        return pltpu.make_async_remote_copy(
            src_ref=src, dst_ref=dst, send_sem=send.at[peer], recv_sem=recv.at[owner], device_id={"dom": peer}, device_id_type=MESH
        )

    def cross_to(src, dst, send, recv, peer):
        return pltpu.make_async_remote_copy(
            src_ref=src, dst_ref=dst, send_sem=send, recv_sem=recv, device_id={"dom": peer}, device_id_type=MESH
        )

    def rows_of(ref, peer):
        return ref.at[span(peer * slots, slots)]

    def send_rows(src, dst, passed, send, recv, pass_recv, first, count):
        for t in range(count):
            peer = first + t
            dx, dy = (peer // 2 // side - cx + side) % side, (peer // 2 % side - cy + side) % side
            detour = (dx % 2 + dy % 2 == 0) & (dx + dy > 0) if side == 4 else None

            def direct(peer=peer):
                cross(rows_of(src, peer), rows_of(dst, q), send, recv, peer, q).start()

            if detour is None:
                pl.when(peer != q)(direct)
                continue
            pl.when((peer != q) & jnp.logical_not(detour))(direct)

            @pl.when(detour)
            def _(peer=peer, dx=dx, dy=dy):
                slot = (dx // 2 + dy // 2 * 2 - 1) * 2 + peer % 2
                pltpu.make_async_remote_copy(
                    src_ref=rows_of(src, peer), dst_ref=passed.at[slot], send_sem=send.at[peer], recv_sem=pass_recv.at[slot],
                    device_id={"dom": at_chip(cx - dx // 2, cy - dy // 2, core)}, device_id_type=MESH,
                ).start()

    def pass_on(dst, passed, send, recv, pass_recv, start):
        if side != 4:
            return

        @pl.loop(0, 6)
        def _(slot):
            kx, ky = (slot // 2 + 1) % 2, (slot // 2 + 1) // 2
            owner = at_chip(cx + kx, cy + ky, core)
            copy = pltpu.make_async_remote_copy(
                src_ref=passed.at[slot], dst_ref=rows_of(dst, owner), send_sem=send.at[slot], recv_sem=recv.at[owner],
                device_id={"dom": at_chip(cx - kx, cy - ky, slot % 2)}, device_id_type=MESH,
            )
            if start:
                pltpu.make_async_remote_copy(
                    src_ref=passed.at[slot], dst_ref=passed.at[slot], send_sem=send.at[slot], recv_sem=pass_recv.at[slot],
                    device_id={"dom": owner}, device_id_type=MESH,
                ).wait_recv()
                copy.start()
            else:
                copy.wait_send()

    def wait_group(ref, send, recv, first, count):
        for t in range(count):
            peer = first + t

            @pl.when(peer != q)
            def _(peer=peer):
                cross(rows_of(ref, peer), rows_of(ref, peer), send, recv, peer, peer).wait_recv()

    def wait_rows(ref, send, recv, what):
        @pl.loop(1, doms)
        def _(i):
            peer = (q + i) % doms
            copy = cross(rows_of(ref, peer), rows_of(ref, peer), send, recv, peer, peer)
            copy.wait_recv() if what == "recv" else copy.wait_send()

    per = CHUNK // slots
    groups = doms // per

    @pl.loop(0, groups)
    def _(n):
        if side == 4:
            step = sum(jnp.where(n == k, v, 0) for k, v in enumerate((5, 4, 1, 3, 2, 7, 6, 0)))
            group = (cx + step // 2) % side * 2 + (cy // 2 + step % 2) % 2
        else:
            group = (q // per + 1 + n) % groups
        lane = lax.broadcasted_iota(jnp.int32, (CHUNK, 128), 1).astype(F32)
        ids = jnp.concatenate(
            [jnp.broadcast_to(cuts[pl.ds(group * (CHUNK // 128) + b, 1), :], (128, 128)).T for b in range(CHUNK // 128)], axis=0
        )
        pick = jnp.concatenate(
            [jnp.where(ids == lane + float(b * 128), 1.0, 0.0).astype(BF16) for b in range(rows // 128)], axis=1
        )
        outgoing[span(group * CHUNK, CHUNK), :] = dot(pick, x[...]).astype(BF16)
        send_rows(outgoing, halo, pass_h, h_s, h_r, hp_r, group * per, per)

    load_l.wait()
    running_sums(order, keep, tiles_l, hist, 0, n_l)
    pass_on(halo, pass_h, hp_s, h_r, hp_r, True)
    z0.wait_recv()
    z4 = ring(part.at[0, pl.ds(0, half)], part.at[2, pl.ds(0, half)], 4, right)
    z4.start()
    z1.wait_recv()
    z5 = ring(part.at[1, pl.ds(half, half)], part.at[2, pl.ds(half, half)], 5, left)
    z5.start()
    place_blocks(last, 0, hist, a_l)

    @pl.loop(0, chunks)
    def _(i):
        at = span(i * CHUNK, CHUNK)
        total[at, :] = dot(a_l[r, at, :], x[...])
        pre_self[at, :] = dot(x[at, :], w_self[...])

    load_h.wait()
    running_sums(order, keep, tiles_h, hist, hist_base, n_h)
    place_blocks(last, a_l.shape[0] * a_l.shape[1] * a_l.shape[2] // (128 * 128), hist, a_h)

    slot_blocks = ret.shape[0] // 128

    @pl.loop(0, rows // 128)
    def _(i):
        ids = (lax.broadcasted_iota(jnp.int32, (128, 128), 0) + i * 128).astype(F32)
        for b in range(slot_blocks):
            tiles_l[i * slot_blocks + b] = jnp.where(cuts[b : b + 1, :] == ids, 1.0, 0.0).astype(BF16)

    z2.wait_recv()
    z3.wait_recv()

    @pl.loop(0, chunks)
    def _(i):
        at = span(i * CHUNK, CHUNK)
        total[at, :] += dot(a_l[left, at, :], part[0]) + dot(a_l[right, at, :], part[1])

    hc = a_h.shape[2]
    h_chunks = a_h.shape[0]
    in_chunk = hc // slots

    def arrival(n):
        if side == 4:
            return (cx + sum(jnp.where(n == k, v, 0) for k, v in enumerate((0, 3, 1, 2)))) % side
        return n

    @pl.loop(0, h_chunks)
    def _(n):
        c = arrival(n)
        wait_group(halo, h_s, h_r, c * in_chunk, in_chunk)

        @pl.loop(0, chunks)
        def _(i):
            at = span(i * CHUNK, CHUNK)
            total[at, :] += dot(a_h[c, at, :], halo[span(c * hc, hc), :])

    z4.wait_recv()
    z5.wait_recv()

    @pl.loop(0, chunks)
    def _(i):
        at = span(i * CHUNK, CHUNK)
        near = (total[at, :] + dot(a_l[far, at, :], part[2])).astype(BF16)
        neigh[at, :] = near
        pre = pre_self[at, :] + dot(near, w_neigh[...])
        sig = jax.nn.sigmoid(pre)
        out[at, :] = (pre * sig).astype(BF16)
        slope = sig * (1.0 + pre * (1.0 - sig))
        g = (cot[at, :].astype(F32) * slope).astype(BF16)
        grad[at, :] = g
        agg_t[:, at] = dot(w_neigh[...], g, TRANS_B).astype(BF16)

    def term(ref, owner):
        @pl.loop(0, chunks)
        def _(i):
            at = span(i * CHUNK, CHUNK)
            ref[:, at] = dot(agg_t[...], a_l[owner, :, at]).astype(BF16)

    f0, f1 = pl.ds(0, fhalf), pl.ds(fhalf, fhalf)
    z6 = ring(t_far.at[f0], via.at[0], 6, right)
    z7 = ring(t_far.at[f1], via.at[1], 7, left)
    for z, f in ((z6, f0), (z7, f1)):

        @pl.loop(0, chunks)
        def _(i, f=f):
            at = span(i * CHUNK, CHUNK)
            t_far[f, at] = dot(agg_t[f, :], a_l[far, :, at]).astype(BF16)

        z.start()

    wait_rows(outgoing, h_s, h_r, "send")

    def back_chunk(n):
        if side == 4:
            c = (cx + sum(jnp.where(n == k, v, 0) for k, v in enumerate((2, 0, 1, 3)))) % side
        else:
            c = (q // in_chunk + 1 + n) % h_chunks
        outgoing[span(c * hc, hc), :] = dot(agg_t[...], a_h[c]).T.astype(BF16)
        return c

    def send_chunk(c):
        send_rows(outgoing, ret, pass_b, b_s, b_r, bp_r, c * in_chunk, in_chunk)

    @pl.loop(0, h_chunks)
    def _(n):
        send_chunk(back_chunk(n))

    term(t_right, right)
    z8 = ring(t_right.at[f1], frm.at[0, f1], 8, right)
    z8.start()
    term(t_left, left)
    z9 = ring(t_left.at[f0], frm.at[1, f0], 9, left)
    z9.start()
    block = width // reps
    for m, lhs in enumerate((x, neigh)):
        for c in range(0, width, CHUNK):
            result = dot(lhs[:, c : c + CHUNK], grad[...], TRANS_A) * scale
            for k in range(CHUNK // block):
                at = (c // block + k) * 2 * block + m * block
                total[at : at + block, :] = result[k * block : (k + 1) * block, :]
    share = 2 * block // doms

    def slices(peer):
        return jnp.concatenate([total[span(e * 2 * block + peer * share, share), :] for e in range(reps)], axis=0)

    @pl.loop(0, chips)
    def _(n):
        w_pair[0, n] = slices(n * 2 + 1 - core).astype(BF16)

    pair = cross_to(w_pair.at[0], w_pair.at[1], p_s.at[0], p_r.at[0], twin)
    pair.start()

    z6.wait_recv()
    t_right[f0, :] = (t_right[f0, :].astype(F32) + via[0].astype(F32)).astype(BF16)
    z10 = ring(t_right.at[f0], frm.at[0, f0], 10, right)
    z10.start()
    z7.wait_recv()
    t_left[f1, :] = (t_left[f1, :].astype(F32) + via[1].astype(F32)).astype(BF16)
    z11 = ring(t_left.at[f1], frm.at[1, f1], 11, left)
    z11.start()
    pair.wait_recv()

    def same_core(i):
        return (chip + i) % chips

    def slice_to(peer, owner):
        return cross_to(w_send.at[peer], w_recv.at[owner], w_s.at[peer], w_r.at[owner], peer * 2 + core)

    @pl.loop(0, chips)
    def _(n):
        peer = same_core(n + 1)
        w_send[peer] = (slices(peer * 2 + core) + w_pair[1, peer].astype(F32)).astype(BF16)

        @pl.when(peer != chip)
        def _():
            slice_to(peer, chip).start()

    w_recv[chip] = w_send[chip]
    pass_on(ret, pass_b, bp_s, b_r, bp_r, True)

    @pl.loop(0, chunks)
    def _(i):
        at = span(i * CHUNK, CHUNK)
        own = dot(agg_t[...], a_l[r, :, at])
        total[at, :] = own.T + dot(grad[at, :], w_self[...], TRANS_B)

    @pl.loop(1, chips)
    def _(i):
        slice_to(same_core(i), same_core(i)).wait_recv()

    summed = lax.fori_loop(
        0, chips, lambda p, acc: acc + w_recv[p].astype(F32), jnp.zeros(w_recv.shape[1:], F32)
    )
    for e in range(reps):
        z_send[e] = summed[e * share : (e + 1) * share, :]

    def small(peer, owner):
        return pltpu.make_async_remote_copy(
            src_ref=z_send.at[peer], dst_ref=z_recv.at[owner], send_sem=q_s.at[peer], recv_sem=q_r.at[owner],
            device_id={"rep": peer}, device_id_type=MESH,
        )

    @pl.loop(1, reps)
    def _(i):
        small((r + i) % reps, r).start()

    z_recv[r] = z_send[r]

    @pl.loop(1, reps)
    def _(i):
        peer = (r + i) % reps
        small(peer, peer).wait_recv()

    done = z_recv[0]
    for e in range(1, reps):
        done += z_recv[e]
    fin[core, chip] = done

    def final_to(peer, owner):
        return cross_to(fin.at[core, owner], fin.at[core, owner], f_s.at[peer], f_r.at[owner], peer * 2 + core)

    @pl.loop(1, chips)
    def _(i):
        final_to(same_core(i), chip).start()

    @pl.loop(0, h_chunks)
    def _(n):
        c = arrival(n)
        wait_group(ret, b_s, b_r, c * in_chunk, in_chunk)
        wide = hc // 128

        @pl.loop(0, chunks)
        def _(i):
            at = span(i * CHUNK, CHUNK)
            pick = jnp.concatenate(
                [
                    jnp.concatenate(
                        [tiles_l[(i * (CHUNK // 128) + k) * slot_blocks + c * wide + b] for b in range(wide)], axis=1
                    )
                    for k in range(CHUNK // 128)
                ],
                axis=0,
            )
            total[at, :] += dot(pick, ret[span(c * hc, hc), :])

    z8.wait_recv()
    z9.wait_recv()

    @pl.loop(0, chunks)
    def _(i):
        at = span(i * CHUNK, CHUNK)
        early = jnp.concatenate([frm[1, f0, at].astype(F32), frm[0, f1, at].astype(F32)], axis=0)
        total[at, :] += early.T

    @pl.loop(1, chips)
    def _(i):
        final_to(same_core(i), same_core(i)).wait_recv()

    to_twin = cross_to(fin.at[core], fin.at[core], p_s.at[1], p_r.at[1], twin)
    to_twin.start()
    z10.wait_recv()
    z11.wait_recv()

    @pl.loop(0, chunks)
    def _(i):
        at = span(i * CHUNK, CHUNK)
        late = jnp.concatenate([frm[0, f0, at].astype(F32), frm[1, f1, at].astype(F32)], axis=0)
        d_x[at, :] = (total[at, :] + late.T).astype(BF16)

    cross_to(fin.at[1 - core], fin.at[1 - core], p_s.at[1], p_r.at[1], twin).wait_recv()

    @pl.loop(0, chips)
    def _(p):
        for c in range(2):
            d_w[span((p * 2 + c) * share, share), :] = fin[c, p]

    for z in (z0, z1, z2, z3, z4, z5, z6, z7, z8, z9, z10, z11):
        z.wait_send()
    wait_rows(outgoing, b_s, b_r, "send")

    pass_on(halo, pass_h, hp_s, h_r, hp_r, False)
    pass_on(ret, pass_b, bp_s, b_r, bp_r, False)
    pair.wait_send()
    to_twin.wait_send()

    @pl.loop(1, chips)
    def _(i):
        slice_to(same_core(i), same_core(i)).wait_send()
        final_to(same_core(i), chip).wait_send()

    @pl.loop(1, reps)
    def _(i):
        peer = (r + i) % reps
        small(peer, peer).wait_send()


def index_kernel(sizes, lr, lc, hr, hk, cut_rows, cut_counts, order, keep, last, cuts, pad, wide):
    ri, cj, hj, n_pos = sizes
    n = pad.shape[1]

    def spread(row):
        return jnp.broadcast_to(row, (n, n))

    i = lax.broadcasted_iota(jnp.int32, (n, n), 0)
    j = lax.broadcasted_iota(jnp.int32, (n, n), 1)
    base = 0
    for m, (row, col, per) in enumerate(((lr, lc, cj), (hr, hk, hj))):
        count = row.shape[1]
        pad[...] = jnp.full(pad.shape, 1e6, F32)
        key = ((col[...] // per) * ri + row[...]) * per + col[...] % per
        pad[0:1, 0:count] = key.astype(F32)
        across = spread(pad[0:1, :])
        down = across.T
        same = across == down
        rank = jnp.sum(jnp.where((across < down) | (same & (j < i)), 1.0, 0.0), axis=1, keepdims=True)
        again = jnp.max(jnp.where(same & (j < i), 1.0, 0.0), axis=1, keepdims=True)
        hit = jnp.where(rank == j.astype(F32), 1.0, 0.0)
        order[0:1, m * n : (m + 1) * n] = jnp.sum(hit * i.astype(F32), axis=0, keepdims=True).astype(jnp.int32)
        keep[0:1, m * n : (m + 1) * n] = jnp.sum(hit * again, axis=0, keepdims=True)
        for p in range(0, n_pos[m], n):
            spot = j.astype(F32) + float(p)
            upto = jnp.sum(jnp.where(down <= spot, 1.0, 0.0), axis=0, keepdims=True)
            full = jnp.max(jnp.where(down == spot, 1.0, 0.0), axis=0, keepdims=True)
            found = jnp.where(full > 0.0, upto - 1.0, float(count)).astype(jnp.int32)
            width = min(n, n_pos[m] - p)
            last[0:1, base + p : base + p + width] = found[:, :width]
        base += n_pos[m]
    groups, slots = cut_rows.shape
    pad[...] = jnp.zeros(pad.shape, F32)
    pad[0:1, 0:groups] = cut_counts[...].astype(F32)
    live = j[:groups, :slots].astype(F32) < spread(pad[0:1, :]).T[:groups, :slots]
    wide[:, 0:slots] = jnp.where(live, cut_rows[...].astype(F32), -1.0)
    even = wide[pl.ds(0, groups // 2, stride=2), :]
    odd = wide[pl.ds(1, groups // 2, stride=2), :]
    lane = lax.broadcasted_iota(jnp.int32, even.shape, 1)
    cuts[...] = jnp.where(lane < slots, even, pltpu.roll(odd, slots, 1))


def deliver_kernel(out, d_x, d_w, out_to, d_x_to, d_self, d_neigh, big, small, sem_in, sem_out):
    rows, half = d_self.shape[0], out.shape[0] // 2
    steps = []
    for m, (a, b) in enumerate(((out, out_to), (d_x, d_x_to))):
        for k in range(2):
            at = pl.ds(k * half, half)
            steps.append((a.at[at], big.at[m, at], b.at[at]))
    for m, b in enumerate((d_self, d_neigh)):
        steps.append((d_w.at[pl.ds(m * rows, rows)], small.at[m], b))
    loads = [pltpu.make_async_copy(a, v, sem_in.at[k]) for k, (a, v, _) in enumerate(steps)]
    stores = [pltpu.make_async_copy(v, b, sem_out.at[k]) for k, (_, v, b) in enumerate(steps)]
    for c in loads:
        c.start()
    for c, d in zip(loads, stores):
        c.wait()
        d.start()
    for d in stores:
        d.wait()


def per_device(
    features, w_self, w_neigh, local_tiles, local_rows, local_cols, halo_tiles, halo_rows, halo_cols, cut_rows, cut_counts, cotangent
):
    rows, width = features.shape
    n_l, size, _ = local_tiles.shape
    n_h = halo_tiles.shape[0]
    reps, doms = lax.axis_size("rep"), lax.axis_size("dom")
    slots = cut_rows.shape[3]
    h_rows = slots * doms
    hc = min(512, h_rows)
    ri, cj, hj = rows // size, rows // size, hc // size
    vm, sm, hbm = (pl.BlockSpec(memory_space=m) for m in (pltpu.VMEM, pltpu.SMEM, pl.ANY))
    n = 128
    n_pos = (reps * ri * cj, ri * h_rows // size)
    order, keep, last, cuts = pl.pallas_call(
        functools.partial(index_kernel, (ri, cj, hj, n_pos)),
        out_shape=(
            jax.ShapeDtypeStruct((1, 2 * n), jnp.int32),
            jax.ShapeDtypeStruct((1, 2 * n), F32),
            jax.ShapeDtypeStruct((1, sum(n_pos)), jnp.int32),
            jax.ShapeDtypeStruct((h_rows // n, n), F32),
        ),
        in_specs=[vm] * 6,
        out_specs=[vm] * 4,
        scratch_shapes=[pltpu.VMEM((8, n), F32), pltpu.VMEM((doms, n), F32)],
    )(
        local_rows.reshape(1, -1), local_cols.reshape(1, -1), halo_rows.reshape(1, -1), halo_cols.reshape(1, -1),
        cut_rows[0, 0], cut_counts[0],
    )
    share = 2 * width // reps // doms
    scale = float(rows * reps * doms) ** (-0.5)
    chips = doms // 2
    dma = lambda n: pltpu.SemaphoreType.DMA((n,))
    out, d_x, d_w = pl.pallas_call(
        functools.partial(layer_kernel, (doms, reps, slots, scale)),
        out_shape=(
            jax.ShapeDtypeStruct((rows, width), BF16),
            jax.ShapeDtypeStruct((rows, width), BF16),
            jax.ShapeDtypeStruct((2 * width // reps, width), F32),
        ),
        in_specs=[sm, sm, sm, vm, vm, vm, vm, vm, hbm, hbm],
        out_specs=[vm, vm, vm],
        scratch_shapes=[
            pltpu.VMEM((n_l, size, size), BF16),
            pltpu.VMEM((n_h, size, size), BF16),
            pltpu.VMEM((max(n_l, n_h) + 1, size, size), BF16),
            pltpu.VMEM((reps, rows, rows), BF16),
            pltpu.VMEM((h_rows // hc, rows, hc), BF16),
            pltpu.VMEM((h_rows, width), BF16),
            pltpu.VMEM((h_rows, width), BF16),
            pltpu.VMEM((3, rows, width), BF16),
            pltpu.VMEM((max(rows, 2 * width), width), F32),
            pltpu.VMEM((rows, width), F32),
            pltpu.VMEM((rows, width), BF16),
            pltpu.VMEM((rows, width), BF16),
            pltpu.VMEM((width, rows), BF16),
            pltpu.VMEM((width, rows), BF16),
            pltpu.VMEM((width, rows), BF16),
            pltpu.VMEM((width, rows), BF16),
            pltpu.VMEM((h_rows, width), BF16),
            pltpu.VMEM((2, width // 2, rows), BF16),
            pltpu.VMEM((2, width, rows), BF16),
            pltpu.VMEM((2, chips, reps * share, width), BF16),
            pltpu.VMEM((chips, reps * share, width), BF16),
            pltpu.VMEM((chips, reps * share, width), BF16),
            pltpu.VMEM((reps, share, width), F32),
            pltpu.VMEM((reps, share, width), F32),
            pltpu.VMEM((2, chips, share, width), F32),
            pltpu.VMEM((6, slots, width), BF16),
            pltpu.VMEM((6, slots, width), BF16),
            dma(2), dma(12), dma(12),
            dma(doms), dma(doms), dma(doms), dma(doms), dma(chips), dma(chips),
            dma(reps), dma(reps), dma(chips), dma(chips), dma(2), dma(2), dma(6), dma(6), dma(6), dma(6),
        ],
        compiler_params=pltpu.CompilerParams(
            collective_id=0, has_side_effects=True, vmem_limit_bytes=60 * 2**20
        ),
    )(order, keep, last, cuts, features, cotangent, w_self, w_neigh, local_tiles, halo_tiles)
    part_w = jax.ShapeDtypeStruct((width // reps, width), F32)
    return pl.pallas_call(
        deliver_kernel,
        out_shape=(
            jax.ShapeDtypeStruct((rows, width), BF16), jax.ShapeDtypeStruct((rows, width), BF16), part_w, part_w,
        ),
        in_specs=[hbm] * 3,
        out_specs=[hbm] * 4,
        scratch_shapes=[
            pltpu.VMEM((2, rows, width), BF16), pltpu.VMEM((2, width // reps, width), F32), dma(6), dma(6),
        ],
    )(out, d_x, d_w)


def solution(mesh):
    both = P(("dom", "rep"), None)
    in_specs = (
        both, P(), P(),
        P(("dom", "rep"), None, None), P(("dom", "rep")), P(("dom", "rep")),
        P(("dom", "rep"), None, None), P(("dom", "rep")), P(("dom", "rep")),
        P("dom", "rep", None, None), P("dom", "rep", None), both,
    )
    out_specs = (both, both, P("rep", None), P("rep", None))
    return jax.shard_map(per_device, mesh=mesh, in_specs=in_specs, out_specs=out_specs, check_vma=False)
```

```python
import functools
import math

import jax
import jax.numpy as jnp
from jax import lax
from jax.experimental import pallas as pl
from jax.experimental.pallas import tpu as pltpu
from jax.sharding import PartitionSpec as P

F32, BF16 = jnp.float32, jnp.bfloat16
TRANS_B = (((1,), (1,)), ((), ()))
TRANS_A = (((0,), (0,)), ((), ()))
MESH = pl.DeviceIdType.MESH
CHUNK = 256


def dot(a, b, dims=None):
    if dims is None:
        return jnp.dot(a, b, preferred_element_type=F32)
    return lax.dot_general(a, b, dims, preferred_element_type=F32)


def span(start, size):
    return pl.ds(pl.multiple_of(start, size), size)


def running_sums(order, keep, tiles, hist, base, count):
    size = tiles.shape[1]
    unroll = 4

    def body(g, total):
        for u in range(unroll):
            k = g * unroll + u
            total = total * keep[0, base + k] + tiles[order[0, base + k]].astype(F32)
            hist[k] = total.astype(BF16)
        return total

    lax.fori_loop(0, count // unroll, body, jnp.zeros((size, size), F32))
    hist[count] = jnp.zeros((size, size), BF16)


def place_blocks(last, base, hist, dense):
    parts, rows, cols = dense.shape
    size = hist.shape[1]
    ri, cj = rows // size, cols // size

    def body(n, carry):
        c, i = n // ri, n % ri
        for j in range(cj):
            dense[c, span(i * size, size), j * size : (j + 1) * size] = hist[last[0, base + n * cj + j]]
        return carry

    lax.fori_loop(0, parts * ri, body, 0)


def layer_kernel(
    sizes,
    order, keep, last, cuts, x, cot_hbm, w_self_hbm, w_neigh_hbm, tiles_l_hbm, tiles_h_hbm,
    out_hbm, d_x, d_w,
    out, cot, w_self, w_neigh, tiles_l, tiles_h, hist, a_l, a_h, outgoing, halo, part, total, pre_self, neigh, grad, agg_t,
    t_far, t_right, t_left, ret, via, frm, w_pair, w_send, w_recv, z_send, z_recv, fin, pass_h, pass_b,
    tile_sem, z_s, z_r, h_s, h_r, b_s, b_r, w_s, w_r, q_s, q_r, f_s, f_r, p_s, p_r, hp_s, hp_r, bp_s, bp_r,
):
    doms, reps, slots, scale = sizes
    rows, width = x.shape
    n_l, n_h = tiles_l.shape[0], tiles_h.shape[0]
    hist_base = order.shape[1] // 2
    half, fhalf = rows // 2, width // 2
    chunks = rows // CHUNK
    q, r = lax.axis_index("dom"), lax.axis_index("rep")
    right, left = (r + 1) % reps, (r + reps - 1) % reps
    far = (r + 2) % reps
    chips = doms // 2
    side = math.isqrt(chips)
    chip, core = q // 2, q % 2
    cx, cy = chip // side, chip % side
    twin = chip * 2 + 1 - core

    def at_chip(ax, ay, c):
        return ((ax + side) % side * side + (ay + side) % side) * 2 + c

    load_l = pltpu.make_async_copy(tiles_l_hbm, tiles_l, tile_sem.at[0])
    load_h = pltpu.make_async_copy(tiles_h_hbm, tiles_h, tile_sem.at[1])
    load_l.start()
    load_h.start()
    loads = [
        pltpu.make_async_copy(a, b, tile_sem.at[2 + k])
        for k, (a, b) in enumerate(((w_self_hbm, w_self), (w_neigh_hbm, w_neigh), (cot_hbm, cot)))
    ]
    for load in loads:
        load.start()
    store_out = pltpu.make_async_copy(out, out_hbm, tile_sem.at[5])

    barrier = pltpu.get_barrier_semaphore()

    @pl.loop(1, doms)
    def _(i):
        pl.semaphore_signal(barrier, inc=1, device_id={"dom": (q + i) % doms}, device_id_type=MESH)

    @pl.loop(1, reps)
    def _(i):
        pl.semaphore_signal(barrier, inc=1, device_id={"rep": (r + i) % reps}, device_id_type=MESH)

    halo[span(q * slots, slots), :] = jnp.zeros((slots, width), BF16)
    ret[span(q * slots, slots), :] = jnp.zeros((slots, width), BF16)
    pl.semaphore_wait(barrier, doms + reps - 2)

    def ring(src, dst, n, to):
        return pltpu.make_async_remote_copy(
            src_ref=src, dst_ref=dst, send_sem=z_s.at[n], recv_sem=z_r.at[n], device_id={"rep": to}, device_id_type=MESH
        )

    x0, x1 = x.at[pl.ds(0, half)], x.at[pl.ds(half, half)]
    z0 = ring(x0, part.at[0, pl.ds(0, half)], 0, right)
    z1 = ring(x1, part.at[1, pl.ds(half, half)], 1, left)
    z2 = ring(x1, part.at[0, pl.ds(half, half)], 2, right)
    z3 = ring(x0, part.at[1, pl.ds(0, half)], 3, left)
    for z in (z0, z1, z2, z3):
        z.start()

    def cross(src, dst, send, recv, peer, owner):
        return pltpu.make_async_remote_copy(
            src_ref=src, dst_ref=dst, send_sem=send.at[peer], recv_sem=recv.at[owner], device_id={"dom": peer}, device_id_type=MESH
        )

    def cross_to(src, dst, send, recv, peer):
        return pltpu.make_async_remote_copy(
            src_ref=src, dst_ref=dst, send_sem=send, recv_sem=recv, device_id={"dom": peer}, device_id_type=MESH
        )

    def rows_of(ref, peer):
        return ref.at[span(peer * slots, slots)]

    def send_rows(src, dst, passed, send, recv, pass_recv, first, count):
        for t in range(count):
            peer = first + t
            dx, dy = (peer // 2 // side - cx + side) % side, (peer // 2 % side - cy + side) % side
            detour = (dx % 2 + dy % 2 == 0) & (dx + dy > 0) if side == 4 else None

            def direct(peer=peer):
                cross(rows_of(src, peer), rows_of(dst, q), send, recv, peer, q).start()

            if detour is None:
                pl.when(peer != q)(direct)
                continue
            pl.when((peer != q) & jnp.logical_not(detour))(direct)

            @pl.when(detour)
            def _(peer=peer, dx=dx, dy=dy):
                slot = (dx // 2 + dy // 2 * 2 - 1) * 2 + peer % 2
                pltpu.make_async_remote_copy(
                    src_ref=rows_of(src, peer), dst_ref=passed.at[slot], send_sem=send.at[peer], recv_sem=pass_recv.at[slot],
                    device_id={"dom": at_chip(cx - dx // 2, cy - dy // 2, core)}, device_id_type=MESH,
                ).start()

    def pass_on(dst, passed, send, recv, pass_recv, start):
        if side != 4:
            return

        @pl.loop(0, 6)
        def _(slot):
            kx, ky = (slot // 2 + 1) % 2, (slot // 2 + 1) // 2
            owner = at_chip(cx + kx, cy + ky, core)
            copy = pltpu.make_async_remote_copy(
                src_ref=passed.at[slot], dst_ref=rows_of(dst, owner), send_sem=send.at[slot], recv_sem=recv.at[owner],
                device_id={"dom": at_chip(cx - kx, cy - ky, slot % 2)}, device_id_type=MESH,
            )
            if start:
                pltpu.make_async_remote_copy(
                    src_ref=passed.at[slot], dst_ref=passed.at[slot], send_sem=send.at[slot], recv_sem=pass_recv.at[slot],
                    device_id={"dom": owner}, device_id_type=MESH,
                ).wait_recv()
                copy.start()
            else:
                copy.wait_send()

    def wait_group(ref, send, recv, first, count):
        for t in range(count):
            peer = first + t

            @pl.when(peer != q)
            def _(peer=peer):
                cross(rows_of(ref, peer), rows_of(ref, peer), send, recv, peer, peer).wait_recv()

    def wait_rows(ref, send, recv, what):
        @pl.loop(1, doms)
        def _(i):
            peer = (q + i) % doms
            copy = cross(rows_of(ref, peer), rows_of(ref, peer), send, recv, peer, peer)
            copy.wait_recv() if what == "recv" else copy.wait_send()

    per = CHUNK // slots
    groups = doms // per

    @pl.loop(0, groups)
    def _(n):
        if side == 4:
            step = sum(jnp.where(n == k, v, 0) for k, v in enumerate((5, 4, 1, 3, 2, 7, 6, 0)))
            group = (cx + step // 2) % side * 2 + (cy // 2 + step % 2) % 2
        else:
            group = (q // per + 1 + n) % groups
        lane = lax.broadcasted_iota(jnp.int32, (CHUNK, 128), 1).astype(F32)
        ids = jnp.concatenate(
            [jnp.broadcast_to(cuts[pl.ds(group * (CHUNK // 128) + b, 1), :], (128, 128)).T for b in range(CHUNK // 128)], axis=0
        )
        pick = jnp.concatenate(
            [jnp.where(ids == lane + float(b * 128), 1.0, 0.0).astype(BF16) for b in range(rows // 128)], axis=1
        )
        outgoing[span(group * CHUNK, CHUNK), :] = dot(pick, x[...]).astype(BF16)
        send_rows(outgoing, halo, pass_h, h_s, h_r, hp_r, group * per, per)

    load_l.wait()
    for load in loads:
        load.wait()
    running_sums(order, keep, tiles_l, hist, 0, n_l)
    pass_on(halo, pass_h, hp_s, h_r, hp_r, True)
    z0.wait_recv()
    z4 = ring(part.at[0, pl.ds(0, half)], part.at[2, pl.ds(0, half)], 4, right)
    z4.start()
    z1.wait_recv()
    z5 = ring(part.at[1, pl.ds(half, half)], part.at[2, pl.ds(half, half)], 5, left)
    z5.start()
    place_blocks(last, 0, hist, a_l)

    @pl.loop(0, chunks)
    def _(i):
        at = span(i * CHUNK, CHUNK)
        total[at, :] = dot(a_l[r, at, :], x[...])
        pre_self[at, :] = dot(x[at, :], w_self[...])

    load_h.wait()
    running_sums(order, keep, tiles_h, hist, hist_base, n_h)
    place_blocks(last, a_l.shape[0] * a_l.shape[1] * a_l.shape[2] // (128 * 128), hist, a_h)

    slot_blocks = ret.shape[0] // 128

    @pl.loop(0, rows // 128)
    def _(i):
        ids = (lax.broadcasted_iota(jnp.int32, (128, 128), 0) + i * 128).astype(F32)
        for b in range(slot_blocks):
            tiles_l[i * slot_blocks + b] = jnp.where(cuts[b : b + 1, :] == ids, 1.0, 0.0).astype(BF16)

    z2.wait_recv()
    z3.wait_recv()

    @pl.loop(0, chunks)
    def _(i):
        at = span(i * CHUNK, CHUNK)
        total[at, :] += dot(a_l[left, at, :], part[0]) + dot(a_l[right, at, :], part[1])

    hc = a_h.shape[2]
    h_chunks = a_h.shape[0]
    in_chunk = hc // slots

    def arrival(n):
        if side == 4:
            return (cx + sum(jnp.where(n == k, v, 0) for k, v in enumerate((0, 3, 1, 2)))) % side
        return n

    @pl.loop(0, h_chunks)
    def _(n):
        c = arrival(n)
        wait_group(halo, h_s, h_r, c * in_chunk, in_chunk)

        @pl.loop(0, chunks)
        def _(i):
            at = span(i * CHUNK, CHUNK)
            total[at, :] += dot(a_h[c, at, :], halo[span(c * hc, hc), :])

    z4.wait_recv()
    z5.wait_recv()

    @pl.loop(0, chunks)
    def _(i):
        at = span(i * CHUNK, CHUNK)
        near = (total[at, :] + dot(a_l[far, at, :], part[2])).astype(BF16)
        neigh[at, :] = near
        pre = pre_self[at, :] + dot(near, w_neigh[...])
        sig = jax.nn.sigmoid(pre)
        out[at, :] = (pre * sig).astype(BF16)
        slope = sig * (1.0 + pre * (1.0 - sig))
        g = (cot[at, :].astype(F32) * slope).astype(BF16)
        grad[at, :] = g
        agg_t[:, at] = dot(w_neigh[...], g, TRANS_B).astype(BF16)

    store_out.start()

    def term(ref, owner):
        @pl.loop(0, chunks)
        def _(i):
            at = span(i * CHUNK, CHUNK)
            ref[:, at] = dot(agg_t[...], a_l[owner, :, at]).astype(BF16)

    f0, f1 = pl.ds(0, fhalf), pl.ds(fhalf, fhalf)
    z6 = ring(t_far.at[f0], via.at[0], 6, right)
    z7 = ring(t_far.at[f1], via.at[1], 7, left)
    for z, f in ((z6, f0), (z7, f1)):

        @pl.loop(0, chunks)
        def _(i, f=f):
            at = span(i * CHUNK, CHUNK)
            t_far[f, at] = dot(agg_t[f, :], a_l[far, :, at]).astype(BF16)

        z.start()

    wait_rows(outgoing, h_s, h_r, "send")

    def back_chunk(n):
        if side == 4:
            c = (cx + sum(jnp.where(n == k, v, 0) for k, v in enumerate((2, 0, 1, 3)))) % side
        else:
            c = (q // in_chunk + 1 + n) % h_chunks
        outgoing[span(c * hc, hc), :] = dot(agg_t[...], a_h[c]).T.astype(BF16)
        return c

    def send_chunk(c):
        send_rows(outgoing, ret, pass_b, b_s, b_r, bp_r, c * in_chunk, in_chunk)

    @pl.loop(0, h_chunks)
    def _(n):
        send_chunk(back_chunk(n))

    term(t_right, right)
    z8 = ring(t_right.at[f1], frm.at[0, f1], 8, right)
    z8.start()
    term(t_left, left)
    z9 = ring(t_left.at[f0], frm.at[1, f0], 9, left)
    z9.start()
    block = width // reps
    for m, lhs in enumerate((x, neigh)):
        for c in range(0, width, CHUNK):
            result = dot(lhs[:, c : c + CHUNK], grad[...], TRANS_A) * scale
            for k in range(CHUNK // block):
                at = (c // block + k) * 2 * block + m * block
                total[at : at + block, :] = result[k * block : (k + 1) * block, :]
    share = 2 * block // doms

    def slices(peer):
        return jnp.concatenate([total[span(e * 2 * block + peer * share, share), :] for e in range(reps)], axis=0)

    @pl.loop(0, chips)
    def _(n):
        w_pair[0, n] = slices(n * 2 + 1 - core).astype(BF16)

    pair = cross_to(w_pair.at[0], w_pair.at[1], p_s.at[0], p_r.at[0], twin)
    pair.start()

    z6.wait_recv()
    t_right[f0, :] = (t_right[f0, :].astype(F32) + via[0].astype(F32)).astype(BF16)
    z10 = ring(t_right.at[f0], frm.at[0, f0], 10, right)
    z10.start()
    z7.wait_recv()
    t_left[f1, :] = (t_left[f1, :].astype(F32) + via[1].astype(F32)).astype(BF16)
    z11 = ring(t_left.at[f1], frm.at[1, f1], 11, left)
    z11.start()
    pair.wait_recv()

    def same_core(i):
        return (chip + i) % chips

    def slice_to(peer, owner):
        return cross_to(w_send.at[peer], w_recv.at[owner], w_s.at[peer], w_r.at[owner], peer * 2 + core)

    @pl.loop(0, chips)
    def _(n):
        peer = same_core(n + 1)
        w_send[peer] = (slices(peer * 2 + core) + w_pair[1, peer].astype(F32)).astype(BF16)

        @pl.when(peer != chip)
        def _():
            slice_to(peer, chip).start()

    w_recv[chip] = w_send[chip]
    pass_on(ret, pass_b, bp_s, b_r, bp_r, True)

    @pl.loop(0, chunks)
    def _(i):
        at = span(i * CHUNK, CHUNK)
        own = dot(agg_t[...], a_l[r, :, at])
        total[at, :] = own.T + dot(grad[at, :], w_self[...], TRANS_B)

    @pl.loop(1, chips)
    def _(i):
        slice_to(same_core(i), same_core(i)).wait_recv()

    summed = lax.fori_loop(
        0, chips, lambda p, acc: acc + w_recv[p].astype(F32), jnp.zeros(w_recv.shape[1:], F32)
    )
    for e in range(reps):
        z_send[e] = summed[e * share : (e + 1) * share, :]

    def small(peer, owner):
        return pltpu.make_async_remote_copy(
            src_ref=z_send.at[peer], dst_ref=z_recv.at[owner], send_sem=q_s.at[peer], recv_sem=q_r.at[owner],
            device_id={"rep": peer}, device_id_type=MESH,
        )

    @pl.loop(1, reps)
    def _(i):
        small((r + i) % reps, r).start()

    z_recv[r] = z_send[r]

    @pl.loop(1, reps)
    def _(i):
        peer = (r + i) % reps
        small(peer, peer).wait_recv()

    done = z_recv[0]
    for e in range(1, reps):
        done += z_recv[e]
    fin[core, chip] = done

    def final_to(peer, owner):
        return cross_to(fin.at[core, owner], fin.at[core, owner], f_s.at[peer], f_r.at[owner], peer * 2 + core)

    @pl.loop(1, chips)
    def _(i):
        final_to(same_core(i), chip).start()

    @pl.loop(0, h_chunks)
    def _(n):
        c = arrival(n)
        wait_group(ret, b_s, b_r, c * in_chunk, in_chunk)
        wide = hc // 128

        @pl.loop(0, chunks)
        def _(i):
            at = span(i * CHUNK, CHUNK)
            pick = jnp.concatenate(
                [
                    jnp.concatenate(
                        [tiles_l[(i * (CHUNK // 128) + k) * slot_blocks + c * wide + b] for b in range(wide)], axis=1
                    )
                    for k in range(CHUNK // 128)
                ],
                axis=0,
            )
            total[at, :] += dot(pick, ret[span(c * hc, hc), :])

    z8.wait_recv()
    z9.wait_recv()

    @pl.loop(0, chunks)
    def _(i):
        at = span(i * CHUNK, CHUNK)
        early = jnp.concatenate([frm[1, f0, at].astype(F32), frm[0, f1, at].astype(F32)], axis=0)
        total[at, :] += early.T

    @pl.loop(1, chips)
    def _(i):
        final_to(same_core(i), same_core(i)).wait_recv()

    to_twin = cross_to(fin.at[core], fin.at[core], p_s.at[1], p_r.at[1], twin)
    to_twin.start()
    z10.wait_recv()
    z11.wait_recv()

    @pl.loop(0, chunks)
    def _(i):
        at = span(i * CHUNK, CHUNK)
        late = jnp.concatenate([frm[0, f0, at].astype(F32), frm[1, f1, at].astype(F32)], axis=0)
        d_x[at, :] = (total[at, :] + late.T).astype(BF16)

    cross_to(fin.at[1 - core], fin.at[1 - core], p_s.at[1], p_r.at[1], twin).wait_recv()

    @pl.loop(0, chips)
    def _(p):
        for c in range(2):
            d_w[span((p * 2 + c) * share, share), :] = fin[c, p]

    store_out.wait()
    for z in (z0, z1, z2, z3, z4, z5, z6, z7, z8, z9, z10, z11):
        z.wait_send()
    wait_rows(outgoing, b_s, b_r, "send")

    pass_on(halo, pass_h, hp_s, h_r, hp_r, False)
    pass_on(ret, pass_b, bp_s, b_r, bp_r, False)
    pair.wait_send()
    to_twin.wait_send()

    @pl.loop(1, chips)
    def _(i):
        slice_to(same_core(i), same_core(i)).wait_send()
        final_to(same_core(i), chip).wait_send()

    @pl.loop(1, reps)
    def _(i):
        peer = (r + i) % reps
        small(peer, peer).wait_send()


def index_kernel(sizes, lr, lc, hr, hk, cut_rows, cut_counts, order, keep, last, cuts, pad, wide):
    ri, cj, hj, n_pos = sizes
    n = pad.shape[1]

    def spread(row):
        return jnp.broadcast_to(row, (n, n))

    i = lax.broadcasted_iota(jnp.int32, (n, n), 0)
    j = lax.broadcasted_iota(jnp.int32, (n, n), 1)
    base = 0
    for m, (row, col, per) in enumerate(((lr, lc, cj), (hr, hk, hj))):
        count = row.shape[1]
        pad[...] = jnp.full(pad.shape, 1e6, F32)
        key = ((col[...] // per) * ri + row[...]) * per + col[...] % per
        pad[0:1, 0:count] = key.astype(F32)
        across = spread(pad[0:1, :])
        down = across.T
        same = across == down
        rank = jnp.sum(jnp.where((across < down) | (same & (j < i)), 1.0, 0.0), axis=1, keepdims=True)
        again = jnp.max(jnp.where(same & (j < i), 1.0, 0.0), axis=1, keepdims=True)
        hit = jnp.where(rank == j.astype(F32), 1.0, 0.0)
        order[0:1, m * n : (m + 1) * n] = jnp.sum(hit * i.astype(F32), axis=0, keepdims=True).astype(jnp.int32)
        keep[0:1, m * n : (m + 1) * n] = jnp.sum(hit * again, axis=0, keepdims=True)
        for p in range(0, n_pos[m], n):
            spot = j.astype(F32) + float(p)
            upto = jnp.sum(jnp.where(down <= spot, 1.0, 0.0), axis=0, keepdims=True)
            full = jnp.max(jnp.where(down == spot, 1.0, 0.0), axis=0, keepdims=True)
            found = jnp.where(full > 0.0, upto - 1.0, float(count)).astype(jnp.int32)
            width = min(n, n_pos[m] - p)
            last[0:1, base + p : base + p + width] = found[:, :width]
        base += n_pos[m]
    groups, slots = cut_rows.shape
    pad[...] = jnp.zeros(pad.shape, F32)
    pad[0:1, 0:groups] = cut_counts[...].astype(F32)
    live = j[:groups, :slots].astype(F32) < spread(pad[0:1, :]).T[:groups, :slots]
    wide[:, 0:slots] = jnp.where(live, cut_rows[...].astype(F32), -1.0)
    even = wide[pl.ds(0, groups // 2, stride=2), :]
    odd = wide[pl.ds(1, groups // 2, stride=2), :]
    lane = lax.broadcasted_iota(jnp.int32, even.shape, 1)
    cuts[...] = jnp.where(lane < slots, even, pltpu.roll(odd, slots, 1))


def deliver_kernel(out, d_x, d_w, out_to, d_x_to, d_self, d_neigh, big, small, sem_in, sem_out):
    rows, half = d_self.shape[0], out.shape[0] // 2
    steps = []
    for m, (a, b) in enumerate(((out, out_to), (d_x, d_x_to))):
        for k in range(2):
            at = pl.ds(k * half, half)
            steps.append((a.at[at], big.at[m, at], b.at[at]))
    for m, b in enumerate((d_self, d_neigh)):
        steps.append((d_w.at[pl.ds(m * rows, rows)], small.at[m], b))
    loads = [pltpu.make_async_copy(a, v, sem_in.at[k]) for k, (a, v, _) in enumerate(steps)]
    stores = [pltpu.make_async_copy(v, b, sem_out.at[k]) for k, (_, v, b) in enumerate(steps)]
    for c in loads:
        c.start()
    for c, d in zip(loads, stores):
        c.wait()
        d.start()
    for d in stores:
        d.wait()


def per_device(
    features, w_self, w_neigh, local_tiles, local_rows, local_cols, halo_tiles, halo_rows, halo_cols, cut_rows, cut_counts, cotangent
):
    rows, width = features.shape
    n_l, size, _ = local_tiles.shape
    n_h = halo_tiles.shape[0]
    reps, doms = lax.axis_size("rep"), lax.axis_size("dom")
    slots = cut_rows.shape[3]
    h_rows = slots * doms
    hc = min(512, h_rows)
    ri, cj, hj = rows // size, rows // size, hc // size
    vm, sm, hbm = (pl.BlockSpec(memory_space=m) for m in (pltpu.VMEM, pltpu.SMEM, pl.ANY))
    n = 128
    n_pos = (reps * ri * cj, ri * h_rows // size)
    order, keep, last, cuts = pl.pallas_call(
        functools.partial(index_kernel, (ri, cj, hj, n_pos)),
        out_shape=(
            jax.ShapeDtypeStruct((1, 2 * n), jnp.int32),
            jax.ShapeDtypeStruct((1, 2 * n), F32),
            jax.ShapeDtypeStruct((1, sum(n_pos)), jnp.int32),
            jax.ShapeDtypeStruct((h_rows // n, n), F32),
        ),
        in_specs=[vm] * 6,
        out_specs=[vm] * 4,
        scratch_shapes=[pltpu.VMEM((8, n), F32), pltpu.VMEM((doms, n), F32)],
    )(
        local_rows.reshape(1, -1), local_cols.reshape(1, -1), halo_rows.reshape(1, -1), halo_cols.reshape(1, -1),
        cut_rows[0, 0], cut_counts[0],
    )
    share = 2 * width // reps // doms
    scale = float(rows * reps * doms) ** (-0.5)
    chips = doms // 2
    dma = lambda n: pltpu.SemaphoreType.DMA((n,))
    out, d_x, d_w = pl.pallas_call(
        functools.partial(layer_kernel, (doms, reps, slots, scale)),
        out_shape=(
            jax.ShapeDtypeStruct((rows, width), BF16),
            jax.ShapeDtypeStruct((rows, width), BF16),
            jax.ShapeDtypeStruct((2 * width // reps, width), F32),
        ),
        in_specs=[sm, sm, sm, vm, vm, hbm, hbm, hbm, hbm, hbm],
        out_specs=[hbm, vm, vm],
        scratch_shapes=[
            pltpu.VMEM((rows, width), BF16),
            pltpu.VMEM((rows, width), BF16),
            pltpu.VMEM((width, width), BF16),
            pltpu.VMEM((width, width), BF16),
            pltpu.VMEM((n_l, size, size), BF16),
            pltpu.VMEM((n_h, size, size), BF16),
            pltpu.VMEM((max(n_l, n_h) + 1, size, size), BF16),
            pltpu.VMEM((reps, rows, rows), BF16),
            pltpu.VMEM((h_rows // hc, rows, hc), BF16),
            pltpu.VMEM((h_rows, width), BF16),
            pltpu.VMEM((h_rows, width), BF16),
            pltpu.VMEM((3, rows, width), BF16),
            pltpu.VMEM((max(rows, 2 * width), width), F32),
            pltpu.VMEM((rows, width), F32),
            pltpu.VMEM((rows, width), BF16),
            pltpu.VMEM((rows, width), BF16),
            pltpu.VMEM((width, rows), BF16),
            pltpu.VMEM((width, rows), BF16),
            pltpu.VMEM((width, rows), BF16),
            pltpu.VMEM((width, rows), BF16),
            pltpu.VMEM((h_rows, width), BF16),
            pltpu.VMEM((2, width // 2, rows), BF16),
            pltpu.VMEM((2, width, rows), BF16),
            pltpu.VMEM((2, chips, reps * share, width), BF16),
            pltpu.VMEM((chips, reps * share, width), BF16),
            pltpu.VMEM((chips, reps * share, width), BF16),
            pltpu.VMEM((reps, share, width), F32),
            pltpu.VMEM((reps, share, width), F32),
            pltpu.VMEM((2, chips, share, width), F32),
            pltpu.VMEM((6, slots, width), BF16),
            pltpu.VMEM((6, slots, width), BF16),
            dma(6), dma(12), dma(12),
            dma(doms), dma(doms), dma(doms), dma(doms), dma(chips), dma(chips),
            dma(reps), dma(reps), dma(chips), dma(chips), dma(2), dma(2), dma(6), dma(6), dma(6), dma(6),
        ],
        compiler_params=pltpu.CompilerParams(
            collective_id=0, has_side_effects=True, vmem_limit_bytes=60 * 2**20
        ),
    )(order, keep, last, cuts, features, cotangent, w_self, w_neigh, local_tiles, halo_tiles)
    part_w = jax.ShapeDtypeStruct((width // reps, width), F32)
    return pl.pallas_call(
        deliver_kernel,
        out_shape=(
            jax.ShapeDtypeStruct((rows, width), BF16), jax.ShapeDtypeStruct((rows, width), BF16), part_w, part_w,
        ),
        in_specs=[hbm] * 3,
        out_specs=[hbm] * 4,
        scratch_shapes=[
            pltpu.VMEM((2, rows, width), BF16), pltpu.VMEM((2, width // reps, width), F32), dma(6), dma(6),
        ],
    )(out, d_x, d_w)


def solution(mesh):
    both = P(("dom", "rep"), None)
    in_specs = (
        both, P(), P(),
        P(("dom", "rep"), None, None), P(("dom", "rep")), P(("dom", "rep")),
        P(("dom", "rep"), None, None), P(("dom", "rep")), P(("dom", "rep")),
        P("dom", "rep", None, None), P("dom", "rep", None), both,
    )
    out_specs = (both, both, P("rep", None), P("rep", None))
    return jax.shard_map(per_device, mesh=mesh, in_specs=in_specs, out_specs=out_specs, check_vma=False)
```
